32 devices in a mesh: group: 4 (over z), dom: 8 (over y, x, core).
Axes of the slice: x: 2, y: 2, z: 4, core: 2. Of those that a mesh axis runs over, the one named last changes fastest.
Arguments:
- query_rows: bfloat16 [24576, 256], P(('group', 'dom')), may hold values from -64 to 64
- key_rows: bfloat16 [24576, 256], P(('group', 'dom')), may hold values from -6 to 6
- value_rows: bfloat16 [24576, 256], P(('group', 'dom')), may hold values from -6 to 6
- out_weight: bfloat16 [256, 256], replicated, may hold values from -1.5 to 1.5
- grad_update: bfloat16 [24576, 256], P(('group', 'dom')), may hold values from -6 to 6
- expander_bias: float32 [8], replicated, may hold values from 1 to 5
- tile_block: int32 [32, 6, 8], P(('group', 'dom')), may hold values from 0 to 13, as said below
- tile_count: int32 [32, 6], P(('group', 'dom')), may hold values from 5 to 8, as said below
- send_block: int32 [32, 8], P(('group', 'dom')), may hold values from 0 to 5
- matching: int32 [32, 3, 768], P(('group', 'dom')), may hold values from 0 to 767, each once within a row
Outputs:
- update: bfloat16 [24576, 256], P(('group', 'dom'))
- query_grad: float32 [24576, 256], P(('group', 'dom'))
- key_grad: float32 [24576, 256], P(('group', 'dom'))
- value_grad: float32 [24576, 256], P(('group', 'dom'))
- weight_grad: float32 [256, 256], replicated
The draws below stay inside these ranges and needn't reach their ends.
Inputs may be any that keep to these rules, and one draw needn't show every extreme that they name: `tile_block`: slot 0 of block b names entry b, the block itself. `tile_count`: some block has all 8 slots in use. `matching`: each row is a permutation of the 768 nodes.
All inputs are finite; a program needn't handle non-finite values.
Results may differ from the reference program's by a relative error of at most 0.035.
Values may be sent and summed in bfloat16 or wider, within the bound.
A program may use at most 128 MiB of HBM per device.

```python
import jax
import jax.numpy as jnp
from jax import lax

D = 256
HEADS = 8
BLOCK = 128
NBLK = 6
TMAX = 8
CAP = 1
NODES = 768
HALO = 8
PARTITIONS = 32
TOTAL = 24576
N_GROUP = 4
N_DOM = 8


def key_parts(key):
    drawn_draw = jax.random.normal(key, (TOTAL, D), jnp.float32)
    return drawn_draw


def slot_counts(key):
    partitions = TOTAL // NODES
    load_limit = jax.random.randint(jax.random.fold_in(key, 41), (partitions, 1), 5, TMAX + 1)
    counts = jax.random.randint(jax.random.fold_in(key, 42), (partitions, NBLK), 5, load_limit + 1)
    return counts.at[0, 0].set(TMAX).astype(jnp.int32)


def draw_key_rows(key, part):
    drawn_draw = key_parts(key)
    return jnp.clip(drawn_draw, -6.0, 6.0).astype(jnp.bfloat16)


def draw_query_rows(key, part):
    key = jax.random.fold_in(key, 2)
    own_draw = jax.random.normal(key, (TOTAL, D), jnp.float32)
    return jnp.clip(own_draw, -6.0, 6.0).astype(jnp.bfloat16)


def draw_tile_block(key, part):
    counts = slot_counts(key)
    key = jax.random.fold_in(key, 3)
    partitions = TOTAL // NODES
    picked_rows = jax.random.randint(jax.random.fold_in(key, 5), (partitions, NBLK, TMAX), 0, NBLK + HALO)
    orders = jax.vmap(lambda one_key: jax.random.permutation(one_key, HALO))(jax.random.split(key, partitions))
    slot_index = jnp.arange(TMAX, dtype=jnp.int32)[None, None, :]
    own_index = jnp.arange(NBLK, dtype=jnp.int32)[None, :, None]
    live = (slot_index >= 1) & (slot_index < counts[:, :, None])
    live_flat = live.reshape(partitions, NBLK * TMAX).astype(jnp.int32)
    rank_flat = jnp.cumsum(live_flat, axis=1) - 1
    halo_pick = jnp.take_along_axis(orders.astype(jnp.int32), jnp.clip(rank_flat, 0, HALO - 1), axis=1)
    halo_pick = (NBLK + halo_pick).reshape(partitions, NBLK, TMAX)
    early = live & (rank_flat.reshape(partitions, NBLK, TMAX) < HALO)
    block_table = jnp.where(early, halo_pick, picked_rows)
    block_table = jnp.where(slot_index == 0, own_index, block_table)
    block_table = block_table.at[0, 0, 1].set(NBLK + HALO - 1)
    return block_table.astype(jnp.int32)


def draw_tile_count(key, part):
    counts = slot_counts(key)
    return counts


def place_ends(array, rng, smallest, top_value):
    place = [jax.random.randint(jax.random.fold_in(rng, axis), (), 0, length) for axis, length in enumerate(array.shape)]
    widest = array.shape.index(max(array.shape))
    next_to = place[:widest] + [(place[widest] + 1) % array.shape[widest]] + place[widest + 1:]
    return array.at[tuple(place)].set(smallest).at[tuple(next_to)].set(top_value)


def shard_levels(rng, shape, cuts, smallest, largest):
    loudness, own = 1.0, jax.random.fold_in(rng, 6)
    for axis_at, parts in cuts:
        steps = jnp.exp(jax.random.uniform(jax.random.fold_in(own, axis_at), (parts,), jnp.float32, smallest / len(cuts), largest / len(cuts)))
        loudness = loudness * jnp.repeat(steps, shape[axis_at] // parts).reshape([-1 if axis == axis_at else 1 for axis in range(len(shape))])
    return loudness


def gaussian(key, dims, deviation, limit, shards=(), held_as=jnp.bfloat16):
    factor_of = shard_levels(key, dims, shards, -0.22, 0.18) if shards else 1.0
    entries = jax.random.normal(key, dims, jnp.float32) * deviation * factor_of
    return jnp.minimum(jnp.maximum(entries, -limit), limit).astype(held_as)


def setup_inputs(seed: int = 0) -> dict:
    key_of = jax.random.split(jax.random.key(seed), 11)
    query_rows = draw_query_rows(jax.random.fold_in(key_of[10], 71), 0)
    key_rows = draw_key_rows(jax.random.fold_in(key_of[10], 71), 0)
    value_rows = gaussian(key_of[2], (TOTAL, D), 1.0, 6.0, ((0, 32),))
    out_weight = gaussian(key_of[3], (D, D), (D // 16) ** -0.5, 1.5)
    grad_update = gaussian(key_of[4], (TOTAL, D), 1.0, 6.0, ((0, 32),))
    expander_bias = jnp.clip(jax.random.uniform(key_of[5], (HEADS,), jnp.float32, 1.0, 5.0), 1.0, 5.0)
    tile_block = draw_tile_block(jax.random.fold_in(key_of[10], 71), 0)
    tile_count = draw_tile_count(jax.random.fold_in(key_of[10], 71), 0)
    send_block = place_ends(jax.random.randint(key_of[8], (PARTITIONS, HALO), 0, NBLK), jax.random.fold_in(key_of[8], 1), 0, NBLK - 1).astype(jnp.int32)
    matching = jax.vmap(lambda own: jax.random.permutation(own, NODES))(jax.random.split(key_of[9], PARTITIONS * 3)).reshape((PARTITIONS, 3, NODES)).astype(jnp.int32)
    return dict(query_rows=query_rows, key_rows=key_rows, value_rows=value_rows, out_weight=out_weight, grad_update=grad_update, expander_bias=expander_bias, tile_block=tile_block, tile_count=tile_count, send_block=send_block, matching=matching)


HIGH = lax.Precision.HIGHEST


def rounded(values_f):
    return lax.optimization_barrier(values_f.astype(jnp.bfloat16)).astype(jnp.float32)


def reference(query_rows, key_rows, value_rows, out_weight, grad_update, expander_bias, tile_block, tile_count, send_block, matching):
    partitions = N_GROUP * N_DOM
    head_dim = D // HEADS
    score_scale = head_dim ** -0.5
    key_blocks = key_rows.reshape(partitions, NBLK, BLOCK, D)
    value_blocks = value_rows.reshape(partitions, NBLK, BLOCK, D)
    key_nodes = key_rows.reshape(partitions, NODES, D)
    value_nodes = value_rows.reshape(partitions, NODES, D)
    query_nodes = query_rows.reshape(partitions, NODES, D)
    grad_nodes = grad_update.reshape(partitions, NODES, D)
    halo_peer = (jnp.arange(HALO) // CAP).astype(jnp.int32)
    halo_slot = (jnp.arange(HALO) % CAP).astype(jnp.int32)

    def halo_sources(partition):
        senders = (partition // N_DOM) * N_DOM + halo_peer
        return senders, (partition % N_DOM) * CAP + halo_slot

    def forward_backward(partition):
        senders, slots_at = halo_sources(partition)
        picked_blocks = send_block[senders, slots_at]
        table_keys = jnp.concatenate([key_blocks[partition], key_blocks[senders, picked_blocks]], axis=0)
        table_values = jnp.concatenate([value_blocks[partition], value_blocks[senders, picked_blocks]], axis=0)
        chosen = tile_block[partition]
        tile_keys = table_keys[chosen].astype(jnp.float32).reshape(NBLK, TMAX, BLOCK, HEADS, head_dim)
        tile_values = table_values[chosen].astype(jnp.float32).reshape(NBLK, TMAX, BLOCK, HEADS, head_dim)
        partners = [partition ^ (partitions >> (turn + 1)) for turn in range(3)]
        far_keys = jnp.stack([key_nodes[partners[turn]][matching[partition, turn]] for turn in range(3)])
        far_keys = far_keys.astype(jnp.float32).reshape(3, NODES, HEADS, head_dim)
        far_values = jnp.stack([value_nodes[partners[turn]][matching[partition, turn]] for turn in range(3)])
        far_values = far_values.astype(jnp.float32).reshape(3, NODES, HEADS, head_dim)
        queries_flat = query_nodes[partition].astype(jnp.float32).reshape(NODES, HEADS, head_dim)
        query_heads = queries_flat.reshape(NBLK, BLOCK, HEADS, head_dim)
        tiles = jnp.einsum("bqhd,btkhd->bqhtk", query_heads, tile_keys) * score_scale
        live_slots = jnp.arange(TMAX)[None, :] < tile_count[partition][:, None]
        tiles = jnp.where(live_slots[:, None, None, :, None], tiles, -jnp.inf)
        edge_scores = jnp.einsum("nhd,mnhd->nhm", queries_flat, far_keys) * score_scale + expander_bias[None, :, None]
        row_top = jnp.maximum(tiles.max(axis=(3, 4)).reshape(NODES, HEADS), edge_scores.max(axis=2))
        top_heads = row_top.reshape(NBLK, BLOCK, HEADS)
        tile_exp = jnp.exp(tiles - top_heads[..., None, None])
        edge_exp = jnp.exp(edge_scores - row_top[..., None])
        row_total = tile_exp.sum(axis=(3, 4)).reshape(NODES, HEADS) + edge_exp.sum(axis=2)
        tile_prob = tile_exp / row_total.reshape(NBLK, BLOCK, HEADS)[..., None, None]
        edge_prob = edge_exp / row_total[..., None]
        tile_weight = rounded(tile_prob)
        edge_weight = rounded(edge_prob)
        mixed = jnp.einsum("bqhtk,btkhd->bqhd", tile_weight, tile_values).reshape(NODES, HEADS, head_dim)
        mixed = mixed + jnp.einsum("nhm,mnhd->nhd", edge_weight, far_values)
        attended = mixed.reshape(NODES, D).astype(jnp.bfloat16)
        update = jnp.dot(attended, out_weight, preferred_element_type=jnp.float32).astype(jnp.bfloat16)
        grads = grad_nodes[partition]
        grad_attended = jnp.dot(grads, out_weight.T, preferred_element_type=jnp.float32).astype(jnp.bfloat16)
        weight_term = jnp.dot(attended.T, grads, preferred_element_type=jnp.float32)
        grad_flat = grad_attended.astype(jnp.float32).reshape(NODES, HEADS, head_dim)
        row_delta = jnp.sum(grad_flat * attended.astype(jnp.float32).reshape(NODES, HEADS, head_dim), axis=2)
        grad_heads = grad_flat.reshape(NBLK, BLOCK, HEADS, head_dim)
        delta_heads = row_delta.reshape(NBLK, BLOCK, HEADS)
        tile_gprob = jnp.einsum("bqhd,btkhd->bqhtk", grad_heads, tile_values)
        tile_gscore = rounded(tile_prob * (tile_gprob - delta_heads[..., None, None]) * score_scale)
        edge_gprob = jnp.einsum("nhd,mnhd->nhm", grad_flat, far_values)
        edge_gscore = rounded(edge_prob * (edge_gprob - row_delta[..., None]) * score_scale)
        query_grad = jnp.einsum("bqhtk,btkhd->bqhd", tile_gscore, tile_keys).reshape(NODES, D)
        query_grad = query_grad + jnp.einsum("nhm,mnhd->nhd", edge_gscore, far_keys).reshape(NODES, D)
        tile_kterms = jnp.einsum("bqhtk,bqhd->btkhd", tile_gscore, query_heads).reshape(NBLK, TMAX, BLOCK, D)
        tile_vterms = jnp.einsum("bqhtk,bqhd->btkhd", tile_weight, grad_heads).reshape(NBLK, TMAX, BLOCK, D)
        slot_onehot = (chosen[..., None] == jnp.arange(NBLK + HALO, dtype=jnp.int32)).astype(jnp.float32)
        table_kgrad = jnp.einsum("btu,btrc->urc", slot_onehot, tile_kterms, precision=HIGH)
        table_vgrad = jnp.einsum("btu,btrc->urc", slot_onehot, tile_vterms, precision=HIGH)
        edge_kterms = jnp.einsum("nhm,nhd->mnhd", edge_gscore, queries_flat).reshape(3, NODES, D)
        edge_vterms = jnp.einsum("nhm,nhd->mnhd", edge_weight, grad_flat).reshape(3, NODES, D)
        placed_key = jnp.stack([jnp.zeros((NODES, D), jnp.bfloat16).at[matching[partition, turn]].set(edge_kterms[turn].astype(jnp.bfloat16)) for turn in range(3)])
        placed_value = jnp.stack([jnp.zeros((NODES, D), jnp.bfloat16).at[matching[partition, turn]].set(edge_vterms[turn].astype(jnp.bfloat16)) for turn in range(3)])
        return (update, query_grad, table_kgrad[:NBLK], table_vgrad[:NBLK],
                table_kgrad[NBLK:].astype(jnp.bfloat16), table_vgrad[NBLK:].astype(jnp.bfloat16),
                placed_key, placed_value, weight_term)

    outputs = lax.map(forward_backward, jnp.arange(partitions, dtype=jnp.int32))
    updates, query_grads, own_key, own_value, halo_key, halo_value, placed_key, placed_value, weight_terms = outputs

    def collect(partition):
        senders, slots_at = halo_sources(partition)
        owner_map = (send_block[partition][:, None] == jnp.arange(NBLK, dtype=jnp.int32)).astype(jnp.float32)
        incoming_key = halo_key[senders, slots_at].astype(jnp.float32)
        incoming_value = halo_value[senders, slots_at].astype(jnp.float32)
        key_sum = own_key[partition] + jnp.einsum("sb,src->brc", owner_map, incoming_key, precision=HIGH)
        value_sum = own_value[partition] + jnp.einsum("sb,src->brc", owner_map, incoming_value, precision=HIGH)
        key_sum = key_sum.reshape(NODES, D)
        value_sum = value_sum.reshape(NODES, D)
        for turn in range(3):
            partner = partition ^ (partitions >> (turn + 1))
            key_sum = key_sum + placed_key[partner, turn].astype(jnp.float32)
            value_sum = value_sum + placed_value[partner, turn].astype(jnp.float32)
        return key_sum, value_sum

    key_grads, value_grads = lax.map(collect, jnp.arange(partitions, dtype=jnp.int32))
    weight_grad = jnp.sum(weight_terms, axis=0) * (TOTAL ** -0.5)
    return (updates.reshape(TOTAL, D), query_grads.reshape(TOTAL, D), key_grads.reshape(TOTAL, D),
            value_grads.reshape(TOTAL, D), weight_grad)
```

```python
import functools
import math

import jax
import jax.numpy as jnp
from jax import lax
from jax.experimental import pallas as pl
from jax.experimental.pallas import tpu as pltpu
from jax.sharding import PartitionSpec as P

LOG2E = math.log2(math.e)
VMEM = pl.BlockSpec(memory_space=pltpu.VMEM)
SMEM = pl.BlockSpec(memory_space=pltpu.SMEM)
F32 = jnp.float32
BF16 = jnp.bfloat16


def params(mib=48):
    return pltpu.CompilerParams(vmem_limit_bytes=mib * 1024 * 1024)


def cost(flops, moved):
    return pl.CostEstimate(flops=int(flops), bytes_accessed=int(moved), transcendentals=0)


def dot(left, right, left_dim=1, right_dim=0):
    return lax.dot_general(
        left, right, (((left_dim,), (right_dim,)), ((), ())), preferred_element_type=F32
    )


def spread(rows, width):
    heads, lanes = rows.shape
    return jnp.concatenate(
        [jnp.broadcast_to(rows[h : h + 1], (width, lanes)) for h in range(heads)], axis=0
    )


def head_sums(product, heads):
    features, lanes = product.shape
    return product.reshape(heads, features // heads, lanes).sum(axis=1)


def pick_kernel(send_ref, k_ref, v_ref, out_ref, *, block):
    def body(s, carry):
        rows = pl.ds(pl.multiple_of(send_ref[s] * block, block), block)
        out_ref[s, pl.ds(0, block), :] = k_ref[rows, :]
        out_ref[s, pl.ds(block, block), :] = v_ref[rows, :]
        return carry

    lax.fori_loop(0, out_ref.shape[0], body, 0)


def fwd_kernel(
    tb_ref, tc_ref, q_ref, k_ref, v_ref, got_ref,
    ot_ref, m_ref, l_ref,
    ktab, vttab, qx, acc, m_s, l_s,
    *, heads, block,
):
    nodes, feat = q_ref.shape
    blocks = nodes // block
    halo = got_ref.shape[0]
    width = feat // heads
    scale2 = width**-0.5 * LOG2E
    groups = heads // 2

    def fill_own(b, carry):
        rows = pl.ds(pl.multiple_of(b * block, block), block)
        ktab[b] = k_ref[rows, :]
        vttab[b] = v_ref[rows, :].T
        return carry

    def fill_halo(s, carry):
        ktab[blocks + s] = got_ref[s, pl.ds(0, block), :]
        vttab[blocks + s] = got_ref[s, pl.ds(block, block), :].T
        return carry

    lax.fori_loop(0, blocks, fill_own, 0)
    lax.fori_loop(0, halo, fill_halo, 0)
    qx[...] = jnp.zeros(qx.shape, qx.dtype)

    def do_block(b, carry):
        rows = pl.ds(pl.multiple_of(b * block, block), block)
        qt = q_ref[rows, :].T
        for h in range(heads):
            qx[h * width : (h + 1) * width, h * block : (h + 1) * block] = qt[
                h * width : (h + 1) * width
            ]
        m_s[...] = jnp.full(m_s.shape, -1e30, F32)
        l_s[...] = jnp.zeros(l_s.shape, F32)
        acc[...] = jnp.zeros(acc.shape, F32)

        def do_tile(t, inner):
            index = tb_ref[b, t]
            k = ktab[index]
            for g in range(groups):
                cols = slice(g * 2 * block, (g + 1) * 2 * block)
                s = dot(k, qx[:, cols])
                old = m_s[:, cols]
                top = jnp.maximum(old, s.max(axis=0, keepdims=True))
                p = jnp.exp2((s - top) * scale2)
                alpha = jnp.exp2((old - top) * scale2)
                m_s[:, cols] = top
                l_s[:, cols] = l_s[:, cols] * alpha + p.sum(axis=0, keepdims=True)
                feats = slice(g * 2 * width, (g + 1) * 2 * width)
                o = dot(vttab[index, feats, :], p.astype(BF16))
                acc[feats, :] = acc[feats, :] * jnp.concatenate(
                    [
                        jnp.broadcast_to(alpha[:, :block], (width, block)),
                        jnp.broadcast_to(alpha[:, block:], (width, block)),
                    ],
                    axis=0,
                ) + jnp.concatenate([o[:width, :block], o[width:, block:]], axis=0)
            return inner

        lax.fori_loop(0, tc_ref[b], do_tile, 0)
        ot_ref[:, rows] = acc[...]
        for h in range(heads):
            m_ref[h : h + 1, rows] = m_s[:, h * block : (h + 1) * block] * (width**-0.5)
            l_ref[h : h + 1, rows] = l_s[:, h * block : (h + 1) * block]
        return carry

    lax.fori_loop(0, blocks, do_block, 0)


def prep_kernel(q_ref, gu_ref, w_ref, qt_ref, gat_ref, ga_ref):
    qt_ref[...] = q_ref[...].T
    ga = dot(gu_ref[...], w_ref[...], 1, 1).astype(BF16)
    ga_ref[...] = ga
    gat_ref[...] = ga.T


def hot(match_row, nodes):
    return (lax.broadcasted_iota(jnp.int32, (nodes, nodes), 0) == match_row).astype(BF16)


def gather_kernel(match_ref, mk_ref, mv_ref, qt_ref, gat_ref, fk_ref, fv_ref, s_ref, dp_ref, *, heads):
    nodes = mk_ref.shape[0]
    onehot = hot(match_ref[...], nodes)
    fk = dot(mk_ref[...].T, onehot)
    fk_ref[...] = fk.astype(BF16)
    s_ref[...] = head_sums(fk * qt_ref[...].astype(F32), heads)
    fv = dot(mv_ref[...].T, onehot)
    fv_ref[...] = fv.astype(BF16)
    dp_ref[...] = head_sums(fv * gat_ref[...].astype(F32), heads)


def merge_kernel(*refs, heads):
    (bias_ref, ot_ref, m_ref, l_ref, gat_ref, gu_ref, w_ref) = refs[:7]
    far = refs[7:19]
    update_ref, term_ref, lse_ref, delta_ref, eq_ref = refs[19:24]
    out = refs[24:]
    feat = ot_ref.shape[0]
    width = feat // heads
    scale = width**-0.5
    scores = [far[4 * e + 2][...] * scale + bias_ref[...] for e in range(3)]
    old = m_ref[...]
    top = functools.reduce(jnp.maximum, scores, old)
    tile_factor = jnp.exp(old - top)
    edge = [jnp.exp(s - top) for s in scores]
    total = l_ref[...] * tile_factor + edge[0] + edge[1] + edge[2]
    probs = [e / total for e in edge]
    weights = [p.astype(BF16).astype(F32) for p in probs]
    mixed = ot_ref[...] * spread(tile_factor / total, width)
    for e in range(3):
        mixed = mixed + spread(weights[e], width) * far[4 * e + 1][...].astype(F32)
    att = mixed.astype(BF16)
    update_ref[...] = dot(att, w_ref[...], 0, 0).astype(BF16)
    term_ref[...] = dot(att, gu_ref[...])
    delta = head_sums(att.astype(F32) * gat_ref[...].astype(F32), heads)
    delta_ref[...] = delta
    lse_ref[...] = top * LOG2E + jnp.log2(total)
    query = None
    for e in range(3):
        ds = (probs[e] * (far[4 * e + 3][...] - delta) * scale).astype(BF16).astype(F32)
        out[2 * e][...] = ds
        out[2 * e + 1][...] = weights[e]
        part = spread(ds, width) * far[4 * e][...].astype(F32)
        query = part if query is None else query + part
    eq_ref[...] = query


def scatter_kernel(match_ref, qt_ref, gat_ref, ds_ref, wt_ref, pk_ref, pv_ref, *, heads):
    feat, nodes = qt_ref.shape
    width = feat // heads
    onehot = hot(match_ref[...], nodes)
    kt = (spread(ds_ref[...], width) * qt_ref[...].astype(F32)).astype(BF16)
    pk_ref[...] = dot(onehot, kt, 1, 1).astype(BF16)
    vt = (spread(wt_ref[...], width) * gat_ref[...].astype(F32)).astype(BF16)
    pv_ref[...] = dot(onehot, vt, 1, 1).astype(BF16)


def bwd_kernel(
    tb_ref, tc_ref, q_ref, k_ref, v_ref, got_ref, qt_ref, gat_ref, ga_ref,
    lse_ref, delta_ref, eq_ref,
    dq_ref, dk_ref, dv_ref, ret_ref,
    ktab, vtab, kttab, qxt, gxt, qx, gx, dkt, dvt, acc, lse_s, delta_s,
    *, heads, block,
):
    nodes, feat = q_ref.shape
    blocks = nodes // block
    halo = got_ref.shape[0]
    width = feat // heads
    scale = width**-0.5
    scale2 = scale * LOG2E
    groups = heads // 2

    def fill_own(b, carry):
        rows = pl.ds(pl.multiple_of(b * block, block), block)
        k = k_ref[rows, :]
        ktab[b] = k
        kttab[b] = k.T
        vtab[b] = v_ref[rows, :]
        return carry

    def fill_halo(s, carry):
        k = got_ref[s, pl.ds(0, block), :]
        ktab[blocks + s] = k
        kttab[blocks + s] = k.T
        vtab[blocks + s] = got_ref[s, pl.ds(block, block), :]
        return carry

    def clear(e, carry):
        dkt[e] = jnp.zeros((block, feat), F32)
        dvt[e] = jnp.zeros((block, feat), F32)
        return carry

    lax.fori_loop(0, blocks, fill_own, 0)
    lax.fori_loop(0, halo, fill_halo, 0)
    lax.fori_loop(0, blocks + halo, clear, 0)
    qxt[...] = jnp.zeros(qxt.shape, qxt.dtype)
    gxt[...] = jnp.zeros(gxt.shape, gxt.dtype)

    def do_block(b, carry):
        rows = pl.ds(pl.multiple_of(b * block, block), block)
        lanes = lax.broadcasted_iota(jnp.int32, (block, feat), 1) // width
        qf = q_ref[rows, :].astype(F32)
        gf = ga_ref[rows, :].astype(F32)
        qt = qt_ref[:, rows]
        gt = gat_ref[:, rows]
        for h in range(heads):
            hs, bs = slice(h * width, (h + 1) * width), slice(h * block, (h + 1) * block)
            qxt[hs, bs] = qt[hs]
            gxt[hs, bs] = gt[hs]
            qx[bs, :] = jnp.where(lanes == h, qf, 0.0).astype(BF16)
            gx[bs, :] = jnp.where(lanes == h, gf, 0.0).astype(BF16)
            lse_s[:, bs] = lse_ref[h : h + 1, rows]
            delta_s[:, bs] = delta_ref[h : h + 1, rows]
        acc[...] = jnp.zeros(acc.shape, F32)

        def do_tile(t, inner):
            index = tb_ref[b, t]
            k = ktab[index]
            v = vtab[index]
            ps, dss = [], []
            for g in range(groups):
                cols = slice(g * 2 * block, (g + 1) * 2 * block)
                s = dot(k, qxt[:, cols])
                p = jnp.exp2(s * scale2 - lse_s[:, cols])
                dp = dot(v, gxt[:, cols])
                ds = (p * (dp - delta_s[:, cols])).astype(BF16)
                ps.append(p.astype(BF16))
                dss.append(ds)
                feats = slice(g * 2 * width, (g + 1) * 2 * width)
                o = dot(kttab[index, feats, :], ds)
                acc[feats, :] += jnp.concatenate([o[:width, :block], o[width:, block:]], axis=0)
            dvt[index] += dot(jnp.concatenate(ps, axis=1), gx[...])
            dkt[index] += dot(jnp.concatenate(dss, axis=1), qx[...])
            return inner

        lax.fori_loop(0, tc_ref[b], do_tile, 0)
        dq_ref[rows, :] = (acc[...] * scale + eq_ref[:, rows]).T
        return carry

    lax.fori_loop(0, blocks, do_block, 0)

    def drain_own(b, carry):
        rows = pl.ds(pl.multiple_of(b * block, block), block)
        dk_ref[rows, :] = dkt[b] * scale
        dv_ref[rows, :] = dvt[b]
        return carry

    def drain_halo(s, carry):
        ret_ref[s, pl.ds(0, block), :] = (dkt[blocks + s] * scale).astype(BF16)
        ret_ref[s, pl.ds(block, block), :] = dvt[blocks + s].astype(BF16)
        return carry

    lax.fori_loop(0, blocks, drain_own, 0)
    lax.fori_loop(0, halo, drain_halo, 0)


def final_kernel(send_ref, dk_ref, dv_ref, home_ref, *refs, block):
    terms, (ok_ref, ov_ref) = refs[:6], refs[6:]
    ok_ref[...] = (
        dk_ref[...] + terms[0][...].astype(F32) + terms[2][...].astype(F32) + terms[4][...].astype(F32)
    )
    ov_ref[...] = (
        dv_ref[...] + terms[1][...].astype(F32) + terms[3][...].astype(F32) + terms[5][...].astype(F32)
    )

    def body(s, carry):
        rows = pl.ds(pl.multiple_of(send_ref[s] * block, block), block)
        ok_ref[rows, :] += home_ref[s, pl.ds(0, block), :].astype(F32)
        ov_ref[rows, :] += home_ref[s, pl.ds(block, block), :].astype(F32)
        return carry

    lax.fori_loop(0, home_ref.shape[0], body, 0)


def call(kernel, name, ins, outs, args, scratch=(), estimate=None, **static):
    return pl.pallas_call(
        functools.partial(kernel, **static),
        name=name,
        in_specs=ins,
        out_specs=[VMEM] * len(outs),
        out_shape=[jax.ShapeDtypeStruct(shape, dtype) for shape, dtype in outs],
        scratch_shapes=list(scratch),
        compiler_params=params(),
        cost_estimate=estimate,
    )(*args)


def from_partner(array, axis, apart):
    return lax.ppermute(array, axis, [(i, i ^ 1 << apart) for i in range(lax.axis_size(axis))])


def shards(
    query_rows, key_rows, value_rows, out_weight, grad_update, expander_bias,
    tile_block, tile_count, send_block, matching,
):
    nodes, feat = query_rows.shape
    heads = expander_bias.shape[0]
    tile_block = tile_block[0]
    tile_count = tile_count[0]
    send_block = send_block[0]
    matching = matching[0]
    blocks, slots = tile_block.shape
    block = nodes // blocks
    halo = send_block.shape[0]
    entries = blocks + halo
    axes = ("group", "dom")
    devices = lax.axis_size(axes)
    top_bit = devices.bit_length() - 1
    wide = heads * block
    tile_flops = 2 * wide * feat * block * blocks * slots

    moved = [
        from_partner((key_rows, value_rows), axes, top_bit - 1 - turn) for turn in range(3)
    ]
    (sent,) = call(
        pick_kernel, "pick", [SMEM, VMEM, VMEM], [((halo, 2 * block, feat), BF16)],
        (send_block, key_rows, value_rows), block=block,
        estimate=cost(0, 4 * halo * block * feat * 2),
    )
    got = lax.all_to_all(sent, "dom", split_axis=0, concat_axis=0, tiled=True)
    qt, gat, ga = call(
        prep_kernel, "prep", [VMEM] * 3,
        [((feat, nodes), BF16), ((feat, nodes), BF16), ((nodes, feat), BF16)],
        (query_rows, grad_update, out_weight),
        estimate=cost(2 * nodes * feat * feat, 10 * nodes * feat),
    )
    ot, top, total = call(
        fwd_kernel, "fwd_tiles", [SMEM, SMEM] + [VMEM] * 4,
        [((feat, nodes), F32), ((heads, nodes), F32), ((heads, nodes), F32)],
        (tile_block, tile_count, query_rows, key_rows, value_rows, got),
        scratch=[
            pltpu.VMEM((entries, block, feat), BF16),
            pltpu.VMEM((entries, feat, block), BF16),
            pltpu.VMEM((feat, wide), BF16),
            pltpu.VMEM((feat, block), F32),
            pltpu.VMEM((1, wide), F32),
            pltpu.VMEM((1, wide), F32),
        ],
        estimate=cost(4 * tile_flops, 8 * nodes * feat * 2),
        heads=heads, block=block,
    )
    rows = [matching[turn : turn + 1] for turn in range(3)]
    far = [None] * 3
    for turn in range(3):
        far[turn] = call(
            gather_kernel, f"gather{turn}", [VMEM] * 5,
            [((feat, nodes), BF16), ((feat, nodes), BF16), ((heads, nodes), F32), ((heads, nodes), F32)],
            (rows[turn], *moved[turn], qt, gat),
            estimate=cost(4 * nodes * nodes * feat, 12 * nodes * feat),
            heads=heads,
        )
    merged = call(
        merge_kernel, "merge", [VMEM] * 19,
        [
            ((nodes, feat), BF16), ((feat, feat), F32), ((heads, nodes), F32),
            ((heads, nodes), F32), ((feat, nodes), F32),
        ] + [((heads, nodes), F32)] * 6,
        (expander_bias.reshape(heads, 1), ot, top, total, gat, grad_update, out_weight,
         *far[0], *far[1], *far[2]),
        estimate=cost(4 * nodes * feat * feat, 24 * nodes * feat),
        heads=heads,
    )
    update, weight_term, lse, delta, edge_query = merged[:5]
    owned = []
    for turn in range(3):
        placed = call(
            scatter_kernel, f"scatter{turn}", [VMEM] * 5,
            [((nodes, feat), BF16), ((nodes, feat), BF16)],
            (rows[turn], qt, gat, merged[5 + 2 * turn], merged[6 + 2 * turn]),
            estimate=cost(4 * nodes * nodes * feat, 10 * nodes * feat),
            heads=heads,
        )
        owned.extend(from_partner(tuple(placed), axes, top_bit - 1 - turn))
    weight_grad = lax.psum(weight_term, axes) * (nodes * devices) ** (-0.5)
    query_grad, own_k, own_v, back = call(
        bwd_kernel, "bwd_tiles", [SMEM, SMEM] + [VMEM] * 10,
        [((nodes, feat), F32), ((nodes, feat), F32), ((nodes, feat), F32), ((halo, 2 * block, feat), BF16)],
        (tile_block, tile_count, query_rows, key_rows, value_rows, got, qt, gat, ga,
         lse, delta, edge_query),
        scratch=[
            pltpu.VMEM((entries, block, feat), BF16),
            pltpu.VMEM((entries, block, feat), BF16),
            pltpu.VMEM((entries, feat, block), BF16),
            pltpu.VMEM((feat, wide), BF16),
            pltpu.VMEM((feat, wide), BF16),
            pltpu.VMEM((wide, feat), BF16),
            pltpu.VMEM((wide, feat), BF16),
            pltpu.VMEM((entries, block, feat), F32),
            pltpu.VMEM((entries, block, feat), F32),
            pltpu.VMEM((feat, block), F32),
            pltpu.VMEM((1, wide), F32),
            pltpu.VMEM((1, wide), F32),
        ],
        estimate=cost(10 * tile_flops, 24 * nodes * feat * 2),
        heads=heads, block=block,
    )
    home = lax.all_to_all(back, "dom", split_axis=0, concat_axis=0, tiled=True)
    key_grad, value_grad = call(
        final_kernel, "final", [SMEM] + [VMEM] * 9,
        [((nodes, feat), F32), ((nodes, feat), F32)],
        (send_block, own_k, own_v, home, *owned),
        estimate=cost(0, 40 * nodes * feat),
        block=block,
    )
    return update, query_grad, key_grad, value_grad, weight_grad


def solution(mesh):
    split = P(("group", "dom"), None)
    split3 = P(("group", "dom"), None, None)
    in_specs = (split, split, split, P(), split, P(), split3, split, split, split3)
    out_specs = (split, split, split, split, P())
    return jax.shard_map(shards, mesh=mesh, in_specs=in_specs, out_specs=out_specs, check_vma=False)
```

```python
import functools
import math

import jax
import jax.numpy as jnp
from jax import lax
from jax.experimental import pallas as pl
from jax.experimental.pallas import tpu as pltpu
from jax.sharding import PartitionSpec as P

LOG2E = math.log2(math.e)
LEAST = 5
VMEM = pl.BlockSpec(memory_space=pltpu.VMEM)
ANY = pl.BlockSpec(memory_space=pl.ANY)
SMEM = pl.BlockSpec(memory_space=pltpu.SMEM)
F32 = jnp.float32
BF16 = jnp.bfloat16


def params(mib=48):
    return pltpu.CompilerParams(vmem_limit_bytes=mib * 1024 * 1024)


def cost(flops, moved):
    return pl.CostEstimate(flops=int(flops), bytes_accessed=int(moved), transcendentals=0)


def dot(left, right, left_dim=1, right_dim=0):
    return lax.dot_general(
        left, right, (((left_dim,), (right_dim,)), ((), ())), preferred_element_type=F32
    )


def spread(rows, width):
    heads, lanes = rows.shape
    return jnp.concatenate(
        [jnp.broadcast_to(rows[h : h + 1], (width, lanes)) for h in range(heads)], axis=0
    )


def head_sums(product, heads):
    features, lanes = product.shape
    return product.reshape(heads, features // heads, lanes).sum(axis=1)


def pick_kernel(send_ref, k_ref, v_ref, out_ref, *, block):
    def body(s, carry):
        rows = pl.ds(pl.multiple_of(send_ref[s] * block, block), block)
        out_ref[s, pl.ds(0, block), :] = k_ref[rows, :]
        out_ref[s, pl.ds(block, block), :] = v_ref[rows, :]
        return carry

    lax.fori_loop(0, out_ref.shape[0], body, 0)


def fwd_kernel(
    tb_ref, tc_ref, q_ref, k_ref, v_ref, got_ref,
    ot_ref, m_ref, l_ref,
    ktab, vttab, kcat, vtcat, qx, m_s, l_s,
    *, heads, block,
):
    nodes, feat = q_ref.shape
    blocks = nodes // block
    halo = got_ref.shape[0]
    width = feat // heads
    scale2 = width**-0.5 * LOG2E
    groups = heads // 2
    slots = tb_ref.shape[1]

    def fill_own(b, carry):
        rows = pl.ds(pl.multiple_of(b * block, block), block)
        ktab[b] = k_ref[rows, :]
        vttab[b] = v_ref[rows, :].T
        return carry

    def fill_halo(s, carry):
        ktab[blocks + s] = got_ref[s, pl.ds(0, block), :]
        vttab[blocks + s] = got_ref[s, pl.ds(block, block), :].T
        return carry

    lax.fori_loop(0, blocks, fill_own, 0)
    lax.fori_loop(0, halo, fill_halo, 0)
    qx[...] = jnp.zeros(qx.shape, qx.dtype)

    def do_block(b, carry):
        rows = pl.ds(pl.multiple_of(b * block, block), block)
        qt = q_ref[rows, :].T
        for h in range(heads):
            qx[h * width : (h + 1) * width, h * block : (h + 1) * block] = qt[
                h * width : (h + 1) * width
            ]
        count = tc_ref[b]
        for t in range(slots):
            index = tb_ref[b, t]
            kcat[t * block : (t + 1) * block, :] = ktab[index]
            vtcat[:, t * block : (t + 1) * block] = vttab[index]
        for g in range(groups):
            cols = slice(g * 2 * block, (g + 1) * 2 * block)
            feats = slice(g * 2 * width, (g + 1) * 2 * width)
            s = dot(kcat[...], qx[:, cols])
            live = [
                s[t * block : (t + 1) * block]
                if t < LEAST
                else jnp.where(t < count, s[t * block : (t + 1) * block], -1e30)
                for t in range(slots)
            ]
            s = jnp.concatenate(live, axis=0)
            top = s.max(axis=0, keepdims=True)
            p = jnp.exp2((s - top) * scale2)
            m_s[:, cols] = top
            l_s[:, cols] = p.sum(axis=0, keepdims=True)
            o = dot(vtcat[feats, :], p.astype(BF16))
            ot_ref[feats, rows] = jnp.concatenate([o[:width, :block], o[width:, block:]], axis=0)
        for h in range(heads):
            m_ref[h : h + 1, rows] = m_s[:, h * block : (h + 1) * block] * (width**-0.5)
            l_ref[h : h + 1, rows] = l_s[:, h * block : (h + 1) * block]
        return carry

    lax.fori_loop(0, blocks, do_block, 0)


def prep_kernel(q_ref, gu_ref, w_ref, qt_ref, gat_ref, ga_ref):
    qt_ref[...] = q_ref[...].T
    ga = dot(gu_ref[...], w_ref[...], 1, 1).astype(BF16)
    ga_ref[...] = ga
    gat_ref[...] = ga.T


def hot(match_row, nodes):
    return (lax.broadcasted_iota(jnp.int32, (nodes, nodes), 0) == match_row).astype(BF16)


def gather_kernel(match_ref, moved_ref, qt_ref, gat_ref, after_ref, fk_ref, fv_ref, s_ref, dp_ref, *, heads):
    nodes = qt_ref.shape[1]
    onehot = hot(match_ref[...], nodes)
    fk = dot(moved_ref[:nodes, :].T, onehot)
    fk_ref[...] = fk.astype(BF16)
    s_ref[...] = head_sums(fk * qt_ref[...].astype(F32), heads)
    fv = dot(moved_ref[nodes:, :].T, onehot)
    fv_ref[...] = fv.astype(BF16)
    dp_ref[...] = head_sums(fv * gat_ref[...].astype(F32), heads)


def merge_kernel(*refs, heads):
    (bias_ref, ot_ref, m_ref, l_ref, gat_ref, gu_ref, w_ref) = refs[:7]
    far = refs[7:19]
    update_ref, term_ref, lse_ref, delta_ref, eq_ref = refs[19:24]
    out = refs[24:]
    feat = ot_ref.shape[0]
    width = feat // heads
    scale = width**-0.5
    scores = [far[4 * e + 2][...] * scale + bias_ref[...] for e in range(3)]
    old = m_ref[...]
    top = functools.reduce(jnp.maximum, scores, old)
    tile_factor = jnp.exp(old - top)
    edge = [jnp.exp(s - top) for s in scores]
    total = l_ref[...] * tile_factor + edge[0] + edge[1] + edge[2]
    probs = [e / total for e in edge]
    weights = [p.astype(BF16).astype(F32) for p in probs]
    mixed = ot_ref[...] * spread(tile_factor / total, width)
    for e in range(3):
        mixed = mixed + spread(weights[e], width) * far[4 * e + 1][...].astype(F32)
    att = mixed.astype(BF16)
    update_ref[...] = dot(att, w_ref[...], 0, 0).astype(BF16)
    term_ref[...] = dot(att, gu_ref[...])
    delta = head_sums(att.astype(F32) * gat_ref[...].astype(F32), heads)
    delta_ref[...] = delta
    lse_ref[...] = top * LOG2E + jnp.log2(total)
    query = None
    for e in range(3):
        ds = (probs[e] * (far[4 * e + 3][...] - delta) * scale).astype(BF16).astype(F32)
        out[2 * e][...] = ds
        out[2 * e + 1][...] = weights[e]
        part = spread(ds, width) * far[4 * e][...].astype(F32)
        query = part if query is None else query + part
    eq_ref[...] = query


def scatter_kernel(match_ref, qt_ref, gat_ref, ds_ref, wt_ref, placed_ref, *, heads):
    feat, nodes = qt_ref.shape
    width = feat // heads
    onehot = hot(match_ref[...], nodes)
    kt = (spread(ds_ref[...], width) * qt_ref[...].astype(F32)).astype(BF16)
    placed_ref[:nodes, :] = dot(onehot, kt, 1, 1).astype(BF16)
    vt = (spread(wt_ref[...], width) * gat_ref[...].astype(F32)).astype(BF16)
    placed_ref[nodes:, :] = dot(onehot, vt, 1, 1).astype(BF16)


def bwd_kernel(
    tb_ref, tc_ref, q_ref, k_ref, v_ref, got_ref, qt_ref, gat_ref, ga_ref,
    lse_ref, delta_ref, eq_ref, after0_ref, after1_ref, after2_ref,
    dq_ref, dk_ref, dv_ref, ret_ref,
    ktab, vtab, kttab, qxt, gxt, qx, gx, dkt, dvt, acc, lse_s, delta_s,
    *, heads, block,
):
    nodes, feat = q_ref.shape
    blocks = nodes // block
    halo = got_ref.shape[0]
    width = feat // heads
    scale = width**-0.5
    scale2 = scale * LOG2E
    groups = heads // 2

    def fill_own(b, carry):
        rows = pl.ds(pl.multiple_of(b * block, block), block)
        k = k_ref[rows, :]
        ktab[b] = k
        kttab[b] = k.T
        vtab[b] = v_ref[rows, :]
        return carry

    def fill_halo(s, carry):
        k = got_ref[s, pl.ds(0, block), :]
        ktab[blocks + s] = k
        kttab[blocks + s] = k.T
        vtab[blocks + s] = got_ref[s, pl.ds(block, block), :]
        return carry

    def clear(e, carry):
        dkt[e] = jnp.zeros((block, feat), F32)
        dvt[e] = jnp.zeros((block, feat), F32)
        return carry

    lax.fori_loop(0, blocks, fill_own, 0)
    lax.fori_loop(0, halo, fill_halo, 0)
    lax.fori_loop(0, blocks + halo, clear, 0)
    qxt[...] = jnp.zeros(qxt.shape, qxt.dtype)
    gxt[...] = jnp.zeros(gxt.shape, gxt.dtype)

    def do_block(b, carry):
        rows = pl.ds(pl.multiple_of(b * block, block), block)
        lanes = lax.broadcasted_iota(jnp.int32, (block, feat), 1) // width
        qf = q_ref[rows, :].astype(F32)
        gf = ga_ref[rows, :].astype(F32)
        qt = qt_ref[:, rows]
        gt = gat_ref[:, rows]
        for h in range(heads):
            hs, bs = slice(h * width, (h + 1) * width), slice(h * block, (h + 1) * block)
            qxt[hs, bs] = qt[hs]
            gxt[hs, bs] = gt[hs]
            qx[bs, :] = jnp.where(lanes == h, qf, 0.0).astype(BF16)
            gx[bs, :] = jnp.where(lanes == h, gf, 0.0).astype(BF16)
            lse_s[:, bs] = lse_ref[h : h + 1, rows]
            delta_s[:, bs] = delta_ref[h : h + 1, rows]
        acc[...] = jnp.zeros(acc.shape, F32)

        count = tc_ref[b]

        def do_pair(pair, inner):
            first, second = tb_ref[b, 2 * pair], tb_ref[b, 2 * pair + 1]
            live = 2 * pair + 1 < count
            k = jnp.concatenate([ktab[first], ktab[second]], axis=0)
            v = jnp.concatenate([vtab[first], vtab[second]], axis=0)
            ps, dss = [], []
            for g in range(groups):
                cols = slice(g * 2 * block, (g + 1) * 2 * block)
                feats = slice(g * 2 * width, (g + 1) * 2 * width)
                s = dot(k, qxt[:, cols])
                p = jnp.exp2(s * scale2 - lse_s[:, cols])
                p = jnp.concatenate([p[:block], jnp.where(live, p[block:], 0.0)], axis=0)
                dp = dot(v, gxt[:, cols])
                ds = (p * (dp - delta_s[:, cols])).astype(BF16)
                ps.append(p.astype(BF16))
                dss.append(ds)
                kt = jnp.concatenate([kttab[first, feats, :], kttab[second, feats, :]], axis=1)
                o = dot(kt, ds)
                acc[feats, :] += jnp.concatenate([o[:width, :block], o[width:, block:]], axis=0)
            dv = dot(jnp.concatenate(ps, axis=1), gx[...])
            dk = dot(jnp.concatenate(dss, axis=1), qx[...])
            dvt[first] += dv[:block]
            dvt[second] += dv[block:]
            dkt[first] += dk[:block]
            dkt[second] += dk[block:]
            return inner

        lax.fori_loop(0, (count + 1) // 2, do_pair, 0)
        dq_ref[rows, :] = (acc[...] * scale + eq_ref[:, rows]).T
        return carry

    lax.fori_loop(0, blocks, do_block, 0)

    def drain_own(b, carry):
        rows = pl.ds(pl.multiple_of(b * block, block), block)
        dk_ref[rows, :] = dkt[b] * scale
        dv_ref[rows, :] = dvt[b]
        return carry

    def drain_halo(s, carry):
        ret_ref[s, pl.ds(0, block), :] = (dkt[blocks + s] * scale).astype(BF16)
        ret_ref[s, pl.ds(block, block), :] = dvt[blocks + s].astype(BF16)
        return carry

    lax.fori_loop(0, blocks, drain_own, 0)
    lax.fori_loop(0, halo, drain_halo, 0)


def final_kernel(send_ref, dk_ref, dv_ref, home_ref, *refs, block):
    terms, (ok_ref, ov_ref) = refs[:3], refs[3:]
    nodes = dk_ref.shape[0]
    ok_ref[...] = dk_ref[...] + sum(term[:nodes, :].astype(F32) for term in terms)
    ov_ref[...] = dv_ref[...] + sum(term[nodes:, :].astype(F32) for term in terms)

    def body(s, carry):
        rows = pl.ds(pl.multiple_of(send_ref[s] * block, block), block)
        ok_ref[rows, :] += home_ref[s, pl.ds(0, block), :].astype(F32)
        ov_ref[rows, :] += home_ref[s, pl.ds(block, block), :].astype(F32)
        return carry

    lax.fori_loop(0, home_ref.shape[0], body, 0)


def call(kernel, name, ins, outs, args, scratch=(), estimate=None, **static):
    return pl.pallas_call(
        functools.partial(kernel, **static),
        name=name,
        in_specs=ins,
        out_specs=[VMEM] * len(outs),
        out_shape=[jax.ShapeDtypeStruct(shape, dtype) for shape, dtype in outs],
        scratch_shapes=list(scratch),
        compiler_params=params(),
        cost_estimate=estimate,
    )(*args)


def from_partner(array, axis, apart):
    return lax.ppermute(array, axis, [(i, i ^ 1 << apart) for i in range(lax.axis_size(axis))])


def reduce_everywhere(term, axes):
    devices = lax.axis_size(axes)
    rows, columns = term.shape
    parts = term.reshape(devices, rows // devices, columns)
    mine = lax.all_to_all(parts, axes, split_axis=0, concat_axis=0, tiled=True).sum(axis=0)
    copies = jnp.broadcast_to(mine[None], parts.shape)
    return lax.all_to_all(copies, axes, split_axis=0, concat_axis=0, tiled=True).reshape(rows, columns)


def shards(
    query_rows, key_rows, value_rows, out_weight, grad_update, expander_bias,
    tile_block, tile_count, send_block, matching,
):
    nodes, feat = query_rows.shape
    heads = expander_bias.shape[0]
    tile_block = tile_block[0]
    tile_count = tile_count[0]
    send_block = send_block[0]
    matching = matching[0]
    blocks, slots = tile_block.shape
    block = nodes // blocks
    halo = send_block.shape[0]
    entries = blocks + halo
    axes = ("group", "dom")
    devices = lax.axis_size(axes)
    top_bit = devices.bit_length() - 1
    wide = heads * block
    tile_flops = 2 * wide * feat * block * blocks * slots

    both = jnp.concatenate([key_rows, value_rows], axis=0)
    moved = [from_partner(both, axes, top_bit - 1 - turn) for turn in range(3)]
    (sent,) = call(
        pick_kernel, "pick", [SMEM, VMEM, VMEM], [((halo, 2 * block, feat), BF16)],
        (send_block, key_rows, value_rows), block=block,
        estimate=cost(0, 4 * halo * block * feat * 2),
    )
    got = lax.all_to_all(sent, "dom", split_axis=0, concat_axis=0, tiled=True)
    qt, gat, ga = call(
        prep_kernel, "prep", [VMEM] * 3,
        [((feat, nodes), BF16), ((feat, nodes), BF16), ((nodes, feat), BF16)],
        (query_rows, grad_update, out_weight),
        estimate=cost(2 * nodes * feat * feat, 10 * nodes * feat),
    )
    ot, top, total = call(
        fwd_kernel, "fwd_tiles", [SMEM, SMEM] + [VMEM] * 4,
        [((feat, nodes), F32), ((heads, nodes), F32), ((heads, nodes), F32)],
        (tile_block, tile_count, query_rows, key_rows, value_rows, got),
        scratch=[
            pltpu.VMEM((entries, block, feat), BF16),
            pltpu.VMEM((entries, feat, block), BF16),
            pltpu.VMEM((slots * block, feat), BF16),
            pltpu.VMEM((feat, slots * block), BF16),
            pltpu.VMEM((feat, wide), BF16),
            pltpu.VMEM((1, wide), F32),
            pltpu.VMEM((1, wide), F32),
        ],
        estimate=cost(8 * tile_flops, 8 * nodes * feat * 2),
        heads=heads, block=block,
    )
    rows = [matching[turn : turn + 1] for turn in range(3)]
    far = [None] * 3
    for turn in range(3):
        far[turn] = call(
            gather_kernel, f"gather{turn}", [VMEM] * 4 + [ANY],
            [((feat, nodes), BF16), ((feat, nodes), BF16), ((heads, nodes), F32), ((heads, nodes), F32)],
            (rows[turn], moved[turn], qt, gat, top),
            estimate=cost(4 * nodes * nodes * feat, 12 * nodes * feat),
            heads=heads,
        )
    merged = call(
        merge_kernel, "merge", [VMEM] * 19,
        [
            ((nodes, feat), BF16), ((feat, feat), F32), ((heads, nodes), F32),
            ((heads, nodes), F32), ((feat, nodes), F32),
        ] + [((heads, nodes), F32)] * 6,
        (expander_bias.reshape(heads, 1), ot, top, total, gat, grad_update, out_weight,
         *far[0], *far[1], *far[2]),
        estimate=cost(4 * nodes * feat * feat, 24 * nodes * feat),
        heads=heads,
    )
    update, weight_term, lse, delta, edge_query = merged[:5]
    owned, ready = [], []
    for turn in range(3):
        (placed,) = call(
            scatter_kernel, f"scatter{turn}", [VMEM] * 5,
            [((2 * nodes, feat), BF16)],
            (rows[turn], qt, gat, merged[5 + 2 * turn], merged[6 + 2 * turn]),
            estimate=cost(4 * nodes * nodes * feat, 10 * nodes * feat),
            heads=heads,
        )
        ready.append(placed)
        owned.append(from_partner(placed, axes, top_bit - 1 - turn))
    weight_grad = reduce_everywhere(weight_term, axes) * (nodes * devices) ** (-0.5)
    query_grad, own_k, own_v, back = call(
        bwd_kernel, "bwd_tiles", [SMEM, SMEM] + [VMEM] * 10 + [ANY] * 3,
        [((nodes, feat), F32), ((nodes, feat), F32), ((nodes, feat), F32), ((halo, 2 * block, feat), BF16)],
        (tile_block, tile_count, query_rows, key_rows, value_rows, got, qt, gat, ga,
         lse, delta, edge_query, *ready),
        scratch=[
            pltpu.VMEM((entries, block, feat), BF16),
            pltpu.VMEM((entries, block, feat), BF16),
            pltpu.VMEM((entries, feat, block), BF16),
            pltpu.VMEM((feat, wide), BF16),
            pltpu.VMEM((feat, wide), BF16),
            pltpu.VMEM((wide, feat), BF16),
            pltpu.VMEM((wide, feat), BF16),
            pltpu.VMEM((entries, block, feat), F32),
            pltpu.VMEM((entries, block, feat), F32),
            pltpu.VMEM((feat, block), F32),
            pltpu.VMEM((1, wide), F32),
            pltpu.VMEM((1, wide), F32),
        ],
        estimate=cost(12 * tile_flops, 24 * nodes * feat * 2),
        heads=heads, block=block,
    )
    home = lax.all_to_all(back, "dom", split_axis=0, concat_axis=0, tiled=True)
    key_grad, value_grad = call(
        final_kernel, "final", [SMEM] + [VMEM] * 6,
        [((nodes, feat), F32), ((nodes, feat), F32)],
        (send_block, own_k, own_v, home, *owned),
        estimate=cost(0, 40 * nodes * feat),
        block=block,
    )
    return update, query_grad, key_grad, value_grad, weight_grad


def solution(mesh):
    split = P(("group", "dom"), None)
    split3 = P(("group", "dom"), None, None)
    in_specs = (split, split, split, P(), split, P(), split3, split, split, split3)
    out_specs = (split, split, split, split, P())
    return jax.shard_map(shards, mesh=mesh, in_specs=in_specs, out_specs=out_specs, check_vma=False)
```

```python
import functools
import math

import jax
import jax.numpy as jnp
from jax import lax
from jax.experimental import pallas as pl
from jax.experimental.pallas import tpu as pltpu
from jax.sharding import PartitionSpec as P

LOG2E = math.log2(math.e)
LEAST = 5
VMEM = pl.BlockSpec(memory_space=pltpu.VMEM)
ANY = pl.BlockSpec(memory_space=pl.ANY)
SMEM = pl.BlockSpec(memory_space=pltpu.SMEM)
F32 = jnp.float32
BF16 = jnp.bfloat16


def params(mib=48):
    return pltpu.CompilerParams(vmem_limit_bytes=mib * 1024 * 1024)


def cost(flops, moved):
    return pl.CostEstimate(flops=int(flops), bytes_accessed=int(moved), transcendentals=0)


def dot(left, right, left_dim=1, right_dim=0):
    return lax.dot_general(
        left, right, (((left_dim,), (right_dim,)), ((), ())), preferred_element_type=F32
    )


def spread(rows, width):
    heads, lanes = rows.shape
    return jnp.concatenate(
        [jnp.broadcast_to(rows[h : h + 1], (width, lanes)) for h in range(heads)], axis=0
    )


def head_sums(product, heads):
    features, lanes = product.shape
    return product.reshape(heads, features // heads, lanes).sum(axis=1)


def pick_kernel(send_ref, both_ref, out_ref, *, block):
    nodes = both_ref.shape[0] // 2

    def body(s, carry):
        start = pl.multiple_of(send_ref[s] * block, block)
        out_ref[s, pl.ds(0, block), :] = both_ref[pl.ds(start, block), :]
        out_ref[s, pl.ds(block, block), :] = both_ref[pl.ds(nodes + start, block), :]
        return carry

    lax.fori_loop(0, out_ref.shape[0], body, 0)


def fwd_kernel(
    tb_ref, tc_ref, q_ref, k_ref, v_ref, got_ref,
    ot_ref, m_ref, l_ref,
    ktab, vttab, kcat, vtcat, qx, m_s, l_s,
    *, heads, block,
):
    nodes, feat = q_ref.shape
    blocks = nodes // block
    halo = got_ref.shape[0]
    width = feat // heads
    scale2 = width**-0.5 * LOG2E
    groups = heads // 2
    slots = tb_ref.shape[1]

    def fill_own(b, carry):
        rows = pl.ds(pl.multiple_of(b * block, block), block)
        ktab[b] = k_ref[rows, :]
        vttab[b] = v_ref[rows, :].T
        return carry

    def fill_halo(s, carry):
        ktab[blocks + s] = got_ref[s, pl.ds(0, block), :]
        vttab[blocks + s] = got_ref[s, pl.ds(block, block), :].T
        return carry

    lax.fori_loop(0, blocks, fill_own, 0)
    lax.fori_loop(0, halo, fill_halo, 0)
    qx[...] = jnp.zeros(qx.shape, qx.dtype)

    def do_block(b, carry):
        rows = pl.ds(pl.multiple_of(b * block, block), block)
        qt = q_ref[rows, :].T
        for h in range(heads):
            qx[h * width : (h + 1) * width, h * block : (h + 1) * block] = qt[
                h * width : (h + 1) * width
            ]
        count = tc_ref[b]
        for t in range(slots):
            index = tb_ref[b, t]
            kcat[t * block : (t + 1) * block, :] = ktab[index]
            vtcat[:, t * block : (t + 1) * block] = vttab[index]
        for g in range(groups):
            cols = slice(g * 2 * block, (g + 1) * 2 * block)
            feats = slice(g * 2 * width, (g + 1) * 2 * width)
            s = dot(kcat[...], qx[:, cols])
            live = [
                s[t * block : (t + 1) * block]
                if t < LEAST
                else jnp.where(t < count, s[t * block : (t + 1) * block], -1e30)
                for t in range(slots)
            ]
            s = jnp.concatenate(live, axis=0)
            top = s.max(axis=0, keepdims=True)
            p = jnp.exp2((s - top) * scale2)
            m_s[:, cols] = top
            l_s[:, cols] = p.sum(axis=0, keepdims=True)
            o = dot(vtcat[feats, :], p.astype(BF16))
            ot_ref[feats, rows] = jnp.concatenate([o[:width, :block], o[width:, block:]], axis=0)
        for h in range(heads):
            m_ref[h : h + 1, rows] = m_s[:, h * block : (h + 1) * block] * (width**-0.5)
            l_ref[h : h + 1, rows] = l_s[:, h * block : (h + 1) * block]
        return carry

    lax.fori_loop(0, blocks, do_block, 0)


def prep_kernel(q_ref, gu_ref, w_ref, qt_ref, gat_ref, ga_ref):
    qt_ref[...] = q_ref[...].T
    ga = dot(gu_ref[...], w_ref[...], 1, 1).astype(BF16)
    ga_ref[...] = ga
    gat_ref[...] = ga.T


def hot(match_row, nodes):
    return (lax.broadcasted_iota(jnp.int32, (nodes, nodes), 0) == match_row).astype(BF16)


def gather_kernel(match_ref, moved_ref, qt_ref, gat_ref, after_ref, fk_ref, fv_ref, s_ref, dp_ref, *, heads):
    nodes = qt_ref.shape[1]
    onehot = hot(match_ref[...], nodes)
    fk = dot(moved_ref[:nodes, :].T, onehot)
    fk_ref[...] = fk.astype(BF16)
    s_ref[...] = head_sums(fk * qt_ref[...].astype(F32), heads)
    fv = dot(moved_ref[nodes:, :].T, onehot)
    fv_ref[...] = fv.astype(BF16)
    dp_ref[...] = head_sums(fv * gat_ref[...].astype(F32), heads)


def merge_kernel(*refs, heads):
    (bias_ref, ot_ref, m_ref, l_ref, gat_ref, gu_ref, w_ref) = refs[:7]
    far = refs[7:19]
    update_ref, term_ref, lse_ref, delta_ref, eq_ref = refs[19:24]
    out = refs[24:]
    feat = ot_ref.shape[0]
    width = feat // heads
    scale = width**-0.5
    scores = [far[4 * e + 2][...] * scale + bias_ref[...] for e in range(3)]
    old = m_ref[...]
    top = functools.reduce(jnp.maximum, scores, old)
    tile_factor = jnp.exp(old - top)
    edge = [jnp.exp(s - top) for s in scores]
    total = l_ref[...] * tile_factor + edge[0] + edge[1] + edge[2]
    probs = [e / total for e in edge]
    weights = [p.astype(BF16).astype(F32) for p in probs]
    mixed = ot_ref[...] * spread(tile_factor / total, width)
    for e in range(3):
        mixed = mixed + spread(weights[e], width) * far[4 * e + 1][...].astype(F32)
    att = mixed.astype(BF16)
    update_ref[...] = dot(att, w_ref[...], 0, 0).astype(BF16)
    term_ref[...] = dot(att, gu_ref[...])
    delta = head_sums(att.astype(F32) * gat_ref[...].astype(F32), heads)
    delta_ref[...] = delta
    lse_ref[...] = top * LOG2E + jnp.log2(total)
    query = None
    for e in range(3):
        ds = (probs[e] * (far[4 * e + 3][...] - delta) * scale).astype(BF16).astype(F32)
        out[2 * e][...] = ds
        out[2 * e + 1][...] = weights[e]
        part = spread(ds, width) * far[4 * e][...].astype(F32)
        query = part if query is None else query + part
    eq_ref[...] = query


def scatter_kernel(match_ref, qt_ref, gat_ref, ds_ref, wt_ref, placed_ref, *, heads):
    feat, nodes = qt_ref.shape
    width = feat // heads
    onehot = hot(match_ref[...], nodes)
    kt = (spread(ds_ref[...], width) * qt_ref[...].astype(F32)).astype(BF16)
    placed_ref[:nodes, :] = dot(onehot, kt, 1, 1).astype(BF16)
    vt = (spread(wt_ref[...], width) * gat_ref[...].astype(F32)).astype(BF16)
    placed_ref[nodes:, :] = dot(onehot, vt, 1, 1).astype(BF16)


def bwd_kernel(
    tb_ref, tc_ref, q_ref, k_ref, v_ref, got_ref, qt_ref, gat_ref, ga_ref,
    lse_ref, delta_ref, eq_ref, after0_ref, after1_ref, after2_ref,
    dq_ref, dk_ref, dv_ref, ret_ref,
    ktab, vtab, kttab, kcat, vcat, ktcat, pbuf, dsbuf, qxt, gxt, qx, gx, dkt, dvt, acc, lse_s, delta_s,
    *, heads, block,
):
    nodes, feat = q_ref.shape
    blocks = nodes // block
    halo = got_ref.shape[0]
    width = feat // heads
    scale = width**-0.5
    scale2 = scale * LOG2E
    groups = heads // 2
    slots = tb_ref.shape[1]

    def fill_own(b, carry):
        rows = pl.ds(pl.multiple_of(b * block, block), block)
        k = k_ref[rows, :]
        ktab[b] = k
        kttab[b] = k.T
        vtab[b] = v_ref[rows, :]
        return carry

    def fill_halo(s, carry):
        k = got_ref[s, pl.ds(0, block), :]
        ktab[blocks + s] = k
        kttab[blocks + s] = k.T
        vtab[blocks + s] = got_ref[s, pl.ds(block, block), :]
        return carry

    def clear(e, carry):
        dkt[e] = jnp.zeros((block, feat), F32)
        dvt[e] = jnp.zeros((block, feat), F32)
        return carry

    lax.fori_loop(0, blocks, fill_own, 0)
    lax.fori_loop(0, halo, fill_halo, 0)
    lax.fori_loop(0, blocks + halo, clear, 0)
    qxt[...] = jnp.zeros(qxt.shape, qxt.dtype)
    gxt[...] = jnp.zeros(gxt.shape, gxt.dtype)

    def do_block(b, carry):
        rows = pl.ds(pl.multiple_of(b * block, block), block)
        lanes = lax.broadcasted_iota(jnp.int32, (block, feat), 1) // width
        qf = q_ref[rows, :].astype(F32)
        gf = ga_ref[rows, :].astype(F32)
        qt = qt_ref[:, rows]
        gt = gat_ref[:, rows]
        for h in range(heads):
            hs, bs = slice(h * width, (h + 1) * width), slice(h * block, (h + 1) * block)
            qxt[hs, bs] = qt[hs]
            gxt[hs, bs] = gt[hs]
            qx[bs, :] = jnp.where(lanes == h, qf, 0.0).astype(BF16)
            gx[bs, :] = jnp.where(lanes == h, gf, 0.0).astype(BF16)
            lse_s[:, bs] = lse_ref[h : h + 1, rows]
            delta_s[:, bs] = delta_ref[h : h + 1, rows]

        count = tc_ref[b]

        for t in range(slots):
            index = tb_ref[b, t]
            part = slice(t * block, (t + 1) * block)
            kcat[part, :] = ktab[index]
            vcat[part, :] = vtab[index]
            ktcat[:, part] = kttab[index]
        for g in range(groups):
            cols = slice(g * 2 * block, (g + 1) * 2 * block)
            feats = slice(g * 2 * width, (g + 1) * 2 * width)
            s = dot(kcat[...], qxt[:, cols])
            p = jnp.exp2(s * scale2 - lse_s[:, cols])
            p = jnp.concatenate(
                [
                    p[t * block : (t + 1) * block]
                    if t < LEAST
                    else jnp.where(t < count, p[t * block : (t + 1) * block], 0.0)
                    for t in range(slots)
                ],
                axis=0,
            )
            dp = dot(vcat[...], gxt[:, cols])
            ds = (p * (dp - delta_s[:, cols])).astype(BF16)
            pbuf[:, cols] = p.astype(BF16)
            dsbuf[:, cols] = ds
            o = dot(ktcat[feats, :], ds)
            acc[feats, :] = jnp.concatenate([o[:width, :block], o[width:, block:]], axis=0)
        dv = dot(pbuf[...], gx[...])
        dk = dot(dsbuf[...], qx[...])
        for t in range(slots):
            index = tb_ref[b, t]
            part = slice(t * block, (t + 1) * block)
            dvt[index] += dv[part]
            dkt[index] += dk[part]
        dq_ref[rows, :] = (acc[...] * scale + eq_ref[:, rows]).T
        return carry

    lax.fori_loop(0, blocks, do_block, 0)

    def drain_own(b, carry):
        rows = pl.ds(pl.multiple_of(b * block, block), block)
        dk_ref[rows, :] = dkt[b] * scale
        dv_ref[rows, :] = dvt[b]
        return carry

    def drain_halo(s, carry):
        ret_ref[s, pl.ds(0, block), :] = (dkt[blocks + s] * scale).astype(BF16)
        ret_ref[s, pl.ds(block, block), :] = dvt[blocks + s].astype(BF16)
        return carry

    lax.fori_loop(0, blocks, drain_own, 0)
    lax.fori_loop(0, halo, drain_halo, 0)


def pass_kernel(back_ref, *refs):
    pass


def final_kernel(send_ref, dk_ref, dv_ref, home_ref, *refs, block):
    terms, (ok_ref, ov_ref) = refs[:3], refs[3:]
    nodes = dk_ref.shape[0]
    ok_ref[...] = dk_ref[...] + sum(term[:nodes, :].astype(F32) for term in terms)
    ov_ref[...] = dv_ref[...] + sum(term[nodes:, :].astype(F32) for term in terms)

    def body(s, carry):
        rows = pl.ds(pl.multiple_of(send_ref[s] * block, block), block)
        ok_ref[rows, :] += home_ref[s, pl.ds(0, block), :].astype(F32)
        ov_ref[rows, :] += home_ref[s, pl.ds(block, block), :].astype(F32)
        return carry

    lax.fori_loop(0, home_ref.shape[0], body, 0)


def call(kernel, name, ins, outs, args, scratch=(), estimate=None, **static):
    return pl.pallas_call(
        functools.partial(kernel, **static),
        name=name,
        in_specs=ins,
        out_specs=[VMEM] * len(outs),
        out_shape=[jax.ShapeDtypeStruct(shape, dtype) for shape, dtype in outs],
        scratch_shapes=list(scratch),
        compiler_params=params(),
        cost_estimate=estimate,
    )(*args)


def from_partner(array, axis, apart):
    return lax.ppermute(array, axis, [(i, i ^ 1 << apart) for i in range(lax.axis_size(axis))])


def reduce_everywhere(term, axes):
    devices = lax.axis_size(axes)
    rows, columns = term.shape
    parts = term.reshape(devices, rows // devices, columns)
    mine = lax.all_to_all(parts, axes, split_axis=0, concat_axis=0, tiled=True).sum(axis=0)
    copies = jnp.broadcast_to(mine[None], parts.shape)
    return lax.all_to_all(copies, axes, split_axis=0, concat_axis=0, tiled=True).reshape(rows, columns)


def shards(
    query_rows, key_rows, value_rows, out_weight, grad_update, expander_bias,
    tile_block, tile_count, send_block, matching,
):
    nodes, feat = query_rows.shape
    heads = expander_bias.shape[0]
    tile_block = tile_block[0]
    tile_count = tile_count[0]
    send_block = send_block[0]
    matching = matching[0]
    blocks, slots = tile_block.shape
    block = nodes // blocks
    halo = send_block.shape[0]
    entries = blocks + halo
    axes = ("group", "dom")
    devices = lax.axis_size(axes)
    top_bit = devices.bit_length() - 1
    wide = heads * block
    tile_flops = 2 * wide * feat * block * blocks * slots

    both = jnp.concatenate([key_rows, value_rows], axis=0)
    moved = [from_partner(both, axes, top_bit - 1 - turn) for turn in range(3)]
    (sent,) = call(
        pick_kernel, "pick", [SMEM, VMEM], [((halo, 2 * block, feat), BF16)],
        (send_block, both), block=block,
        estimate=cost(0, 4 * halo * block * feat * 2),
    )
    got = lax.all_to_all(sent, "dom", split_axis=0, concat_axis=0, tiled=True)
    qt, gat, ga = call(
        prep_kernel, "prep", [VMEM] * 3,
        [((feat, nodes), BF16), ((feat, nodes), BF16), ((nodes, feat), BF16)],
        (query_rows, grad_update, out_weight),
        estimate=cost(2 * nodes * feat * feat, 10 * nodes * feat),
    )
    ot, top, total = call(
        fwd_kernel, "fwd_tiles", [SMEM, SMEM] + [VMEM] * 4,
        [((feat, nodes), F32), ((heads, nodes), F32), ((heads, nodes), F32)],
        (tile_block, tile_count, query_rows, key_rows, value_rows, got),
        scratch=[
            pltpu.VMEM((entries, block, feat), BF16),
            pltpu.VMEM((entries, feat, block), BF16),
            pltpu.VMEM((slots * block, feat), BF16),
            pltpu.VMEM((feat, slots * block), BF16),
            pltpu.VMEM((feat, wide), BF16),
            pltpu.VMEM((1, wide), F32),
            pltpu.VMEM((1, wide), F32),
        ],
        estimate=cost(tile_flops / 2, nodes * feat),
        heads=heads, block=block,
    )
    rows = [matching[turn : turn + 1] for turn in range(3)]
    far = [None] * 3
    for turn in range(3):
        far[turn] = call(
            gather_kernel, f"gather{turn}", [VMEM] * 4 + [ANY],
            [((feat, nodes), BF16), ((feat, nodes), BF16), ((heads, nodes), F32), ((heads, nodes), F32)],
            (rows[turn], moved[turn], qt, gat, top),
            estimate=cost(4 * nodes * nodes * feat, 12 * nodes * feat),
            heads=heads,
        )
    merged = call(
        merge_kernel, "merge", [VMEM] * 19,
        [
            ((nodes, feat), BF16), ((feat, feat), F32), ((heads, nodes), F32),
            ((heads, nodes), F32), ((feat, nodes), F32),
        ] + [((heads, nodes), F32)] * 6,
        (expander_bias.reshape(heads, 1), ot, top, total, gat, grad_update, out_weight,
         *far[0], *far[1], *far[2]),
        estimate=cost(4 * nodes * feat * feat, 24 * nodes * feat),
        heads=heads,
    )
    update, weight_term, lse, delta, edge_query = merged[:5]
    owned, ready = [], []
    for turn in range(3):
        (placed,) = call(
            scatter_kernel, f"scatter{turn}", [VMEM] * 5,
            [((2 * nodes, feat), BF16)],
            (rows[turn], qt, gat, merged[5 + 2 * turn], merged[6 + 2 * turn]),
            estimate=cost(4 * nodes * nodes * feat, 10 * nodes * feat),
            heads=heads,
        )
        ready.append(placed)
        owned.append(from_partner(placed, axes, top_bit - 1 - turn))
    weight_grad = reduce_everywhere(weight_term, axes) * (nodes * devices) ** (-0.5)
    query_grad, own_k, own_v, back = call(
        bwd_kernel, "bwd_tiles", [SMEM, SMEM] + [VMEM] * 10 + [ANY] * 3,
        [((nodes, feat), F32), ((nodes, feat), F32), ((nodes, feat), F32), ((halo, 2 * block, feat), BF16)],
        (tile_block, tile_count, query_rows, key_rows, value_rows, got, qt, gat, ga,
         lse, delta, edge_query, *ready),
        scratch=[
            pltpu.VMEM((entries, block, feat), BF16),
            pltpu.VMEM((entries, block, feat), BF16),
            pltpu.VMEM((entries, feat, block), BF16),
            pltpu.VMEM((slots * block, feat), BF16),
            pltpu.VMEM((slots * block, feat), BF16),
            pltpu.VMEM((feat, slots * block), BF16),
            pltpu.VMEM((slots * block, wide), BF16),
            pltpu.VMEM((slots * block, wide), BF16),
            pltpu.VMEM((feat, wide), BF16),
            pltpu.VMEM((feat, wide), BF16),
            pltpu.VMEM((wide, feat), BF16),
            pltpu.VMEM((wide, feat), BF16),
            pltpu.VMEM((entries, block, feat), F32),
            pltpu.VMEM((entries, block, feat), F32),
            pltpu.VMEM((feat, block), F32),
            pltpu.VMEM((1, wide), F32),
            pltpu.VMEM((1, wide), F32),
        ],
        estimate=cost(tile_flops / 2, nodes * feat),
        heads=heads, block=block,
    )
    back = pl.pallas_call(
        pass_kernel,
        name="after_terms",
        in_specs=[ANY] * 4,
        out_specs=ANY,
        out_shape=jax.ShapeDtypeStruct(back.shape, back.dtype),
        input_output_aliases={0: 0},
        cost_estimate=cost(0, 0),
    )(back, *owned)
    home = lax.all_to_all(back, "dom", split_axis=0, concat_axis=0, tiled=True)
    key_grad, value_grad = call(
        final_kernel, "final", [SMEM] + [VMEM] * 6,
        [((nodes, feat), F32), ((nodes, feat), F32)],
        (send_block, own_k, own_v, home, *owned),
        estimate=cost(0, 40 * nodes * feat),
        block=block,
    )
    return update, query_grad, key_grad, value_grad, weight_grad


def solution(mesh):
    split = P(("group", "dom"), None)
    split3 = P(("group", "dom"), None, None)
    in_specs = (split, split, split, P(), split, P(), split3, split, split, split3)
    out_specs = (split, split, split, split, P())
    return jax.shard_map(shards, mesh=mesh, in_specs=in_specs, out_specs=out_specs, check_vma=False)
```

```python
import functools
import math

import jax
import jax.numpy as jnp
from jax import lax
from jax.experimental import pallas as pl
from jax.experimental.pallas import tpu as pltpu
from jax.sharding import PartitionSpec as P

LOG2E = math.log2(math.e)
LEAST = 5
VMEM = pl.BlockSpec(memory_space=pltpu.VMEM)
ANY = pl.BlockSpec(memory_space=pl.ANY)
SMEM = pl.BlockSpec(memory_space=pltpu.SMEM)
F32 = jnp.float32
BF16 = jnp.bfloat16


def params(mib):
    return pltpu.CompilerParams(vmem_limit_bytes=mib * 1024 * 1024)


def cost(flops, moved):
    return pl.CostEstimate(flops=int(flops), bytes_accessed=int(moved), transcendentals=0)


def dot(left, right, left_dim=1, right_dim=0):
    return lax.dot_general(
        left, right, (((left_dim,), (right_dim,)), ((), ())), preferred_element_type=F32
    )


def spread(rows, width):
    heads, lanes = rows.shape
    return jnp.concatenate(
        [jnp.broadcast_to(rows[h : h + 1], (width, lanes)) for h in range(heads)], axis=0
    )


def head_sums(product, heads):
    features, lanes = product.shape
    return product.reshape(heads, features // heads, lanes).sum(axis=1)


def pick_kernel(send_ref, both_ref, out_ref, *, block):
    nodes = both_ref.shape[0] // 2

    def body(s, carry):
        start = pl.multiple_of(send_ref[s] * block, block)
        out_ref[s, pl.ds(0, block), :] = both_ref[pl.ds(start, block), :]
        out_ref[s, pl.ds(block, block), :] = both_ref[pl.ds(nodes + start, block), :]
        return carry

    lax.fori_loop(0, out_ref.shape[0], body, 0)


def fwd_kernel(
    tb_ref, tc_ref, q_ref, k_ref, v_ref, got_ref,
    ot_ref, m_ref, l_ref,
    ktab, vttab, kcat, vtcat, qx, m_s, l_s,
    *, heads, block,
):
    nodes, feat = q_ref.shape
    blocks = nodes // block
    halo = got_ref.shape[0]
    width = feat // heads
    scale2 = width**-0.5 * LOG2E
    groups = heads // 2
    slots = tb_ref.shape[1]

    def fill_own(b, carry):
        rows = pl.ds(pl.multiple_of(b * block, block), block)
        ktab[b] = k_ref[rows, :]
        vttab[b] = v_ref[rows, :].T
        return carry

    def fill_halo(s, carry):
        ktab[blocks + s] = got_ref[s, pl.ds(0, block), :]
        vttab[blocks + s] = got_ref[s, pl.ds(block, block), :].T
        return carry

    lax.fori_loop(0, blocks, fill_own, 0)
    lax.fori_loop(0, halo, fill_halo, 0)
    qx[...] = jnp.zeros(qx.shape, qx.dtype)

    def do_block(b, carry):
        rows = pl.ds(pl.multiple_of(b * block, block), block)
        qt = q_ref[rows, :].T
        for h in range(heads):
            qx[h * width : (h + 1) * width, h * block : (h + 1) * block] = qt[
                h * width : (h + 1) * width
            ]
        count = tc_ref[b]
        for t in range(slots):
            index = tb_ref[b, t]
            kcat[t * block : (t + 1) * block, :] = ktab[index]
            vtcat[:, t * block : (t + 1) * block] = vttab[index]
        for g in range(groups):
            cols = slice(g * 2 * block, (g + 1) * 2 * block)
            feats = slice(g * 2 * width, (g + 1) * 2 * width)
            s = dot(kcat[...], qx[:, cols])
            live = [
                s[t * block : (t + 1) * block]
                if t < LEAST
                else jnp.where(t < count, s[t * block : (t + 1) * block], -1e30)
                for t in range(slots)
            ]
            s = jnp.concatenate(live, axis=0)
            top = s.max(axis=0, keepdims=True)
            p = jnp.exp2((s - top) * scale2)
            m_s[:, cols] = top
            l_s[:, cols] = p.sum(axis=0, keepdims=True)
            o = dot(vtcat[feats, :], p.astype(BF16))
            ot_ref[feats, rows] = jnp.concatenate([o[:width, :block], o[width:, block:]], axis=0)
        for h in range(heads):
            m_ref[h : h + 1, rows] = m_s[:, h * block : (h + 1) * block] * (width**-0.5)
            l_ref[h : h + 1, rows] = l_s[:, h * block : (h + 1) * block]
        return carry

    lax.fori_loop(0, blocks, do_block, 0)


def prep_kernel(q_ref, gu_ref, w_ref, qt_ref, gat_ref, ga_ref):
    qt_ref[...] = q_ref[...].T
    ga = dot(gu_ref[...], w_ref[...], 1, 1).astype(BF16)
    ga_ref[...] = ga
    gat_ref[...] = ga.T


def hot(match_row, nodes):
    return (lax.broadcasted_iota(jnp.int32, (nodes, nodes), 0) == match_row).astype(BF16)


def gather_kernel(match_ref, moved_ref, qt_ref, gat_ref, after_ref, fk_ref, fv_ref, s_ref, dp_ref, *, heads):
    nodes = qt_ref.shape[1]
    onehot = hot(match_ref[...], nodes)
    fk = dot(moved_ref[:nodes, :].T, onehot)
    fk_ref[...] = fk.astype(BF16)
    s_ref[...] = head_sums(fk * qt_ref[...].astype(F32), heads)
    fv = dot(moved_ref[nodes:, :].T, onehot)
    fv_ref[...] = fv.astype(BF16)
    dp_ref[...] = head_sums(fv * gat_ref[...].astype(F32), heads)


def merge_kernel(*refs, heads):
    (bias_ref, ot_ref, m_ref, l_ref, gat_ref, w_ref) = refs[:6]
    far = refs[6:18]
    update_ref, att_ref, lse_ref, delta_ref, eq_ref = refs[18:23]
    out = refs[23:]
    feat = ot_ref.shape[0]
    width = feat // heads
    scale = width**-0.5
    scores = [far[4 * e + 2][...] * scale + bias_ref[...] for e in range(3)]
    old = m_ref[...]
    top = functools.reduce(jnp.maximum, scores, old)
    tile_factor = jnp.exp(old - top)
    edge = [jnp.exp(s - top) for s in scores]
    total = l_ref[...] * tile_factor + edge[0] + edge[1] + edge[2]
    probs = [e / total for e in edge]
    weights = [p.astype(BF16).astype(F32) for p in probs]
    mixed = ot_ref[...] * spread(tile_factor / total, width)
    for e in range(3):
        mixed = mixed + spread(weights[e], width) * far[4 * e + 1][...].astype(F32)
    att = mixed.astype(BF16)
    update_ref[...] = dot(att, w_ref[...], 0, 0).astype(BF16)
    att_ref[...] = att
    delta = head_sums(att.astype(F32) * gat_ref[...].astype(F32), heads)
    delta_ref[...] = delta
    lse_ref[...] = top * LOG2E + jnp.log2(total)
    query = None
    for e in range(3):
        ds = (probs[e] * (far[4 * e + 3][...] - delta) * scale).astype(BF16).astype(F32)
        out[2 * e][...] = ds
        out[2 * e + 1][...] = weights[e]
        part = spread(ds, width) * far[4 * e][...].astype(F32)
        query = part if query is None else query + part
    eq_ref[...] = query


def weight_kernel(att_ref, gu_ref, after_ref, term_ref):
    term_ref[...] = dot(att_ref[...], gu_ref[...])


def scatter_kernel(match_ref, qt_ref, gat_ref, ds_ref, wt_ref, after_ref, placed_ref, *, heads):
    feat, nodes = qt_ref.shape
    width = feat // heads
    onehot = hot(match_ref[...], nodes)
    kt = (spread(ds_ref[...], width) * qt_ref[...].astype(F32)).astype(BF16)
    placed_ref[:nodes, :] = dot(onehot, kt, 1, 1).astype(BF16)
    vt = (spread(wt_ref[...], width) * gat_ref[...].astype(F32)).astype(BF16)
    placed_ref[nodes:, :] = dot(onehot, vt, 1, 1).astype(BF16)


def bwd_kernel(
    tb_ref, tc_ref, q_ref, k_ref, v_ref, got_ref, qt_ref, gat_ref, ga_ref,
    lse_ref, delta_ref, eq_ref, after0_ref, after1_ref, after2_ref,
    dq_ref, dk_ref, dv_ref, ret_ref,
    ktab, vtab, kttab, kcat, vcat, ktcat, pbuf, dsbuf, qxt, gxt, qx, gx, dkt, dvt, acc, lse_s, delta_s,
    *, heads, block,
):
    nodes, feat = q_ref.shape
    blocks = nodes // block
    halo = got_ref.shape[0]
    width = feat // heads
    scale = width**-0.5
    scale2 = scale * LOG2E
    groups = heads // 2
    slots = tb_ref.shape[1]

    def fill_own(b, carry):
        rows = pl.ds(pl.multiple_of(b * block, block), block)
        k = k_ref[rows, :]
        ktab[b] = k
        kttab[b] = k.T
        vtab[b] = v_ref[rows, :]
        return carry

    def fill_halo(s, carry):
        k = got_ref[s, pl.ds(0, block), :]
        ktab[blocks + s] = k
        kttab[blocks + s] = k.T
        vtab[blocks + s] = got_ref[s, pl.ds(block, block), :]
        return carry

    def clear(e, carry):
        dkt[e] = jnp.zeros((block, feat), F32)
        dvt[e] = jnp.zeros((block, feat), F32)
        return carry

    lax.fori_loop(0, blocks, fill_own, 0)
    lax.fori_loop(0, halo, fill_halo, 0)
    lax.fori_loop(0, blocks + halo, clear, 0)
    qxt[...] = jnp.zeros(qxt.shape, qxt.dtype)
    gxt[...] = jnp.zeros(gxt.shape, gxt.dtype)

    def do_block(b, carry):
        rows = pl.ds(pl.multiple_of(b * block, block), block)
        lanes = lax.broadcasted_iota(jnp.int32, (block, feat), 1) // width
        qf = q_ref[rows, :].astype(F32)
        gf = ga_ref[rows, :].astype(F32)
        qt = qt_ref[:, rows]
        gt = gat_ref[:, rows]
        for h in range(heads):
            hs, bs = slice(h * width, (h + 1) * width), slice(h * block, (h + 1) * block)
            qxt[hs, bs] = qt[hs]
            gxt[hs, bs] = gt[hs]
            qx[bs, :] = jnp.where(lanes == h, qf, 0.0).astype(BF16)
            gx[bs, :] = jnp.where(lanes == h, gf, 0.0).astype(BF16)
            lse_s[:, bs] = lse_ref[h : h + 1, rows]
            delta_s[:, bs] = delta_ref[h : h + 1, rows]

        count = tc_ref[b]

        for t in range(slots):
            index = tb_ref[b, t]
            part = slice(t * block, (t + 1) * block)
            kcat[part, :] = ktab[index]
            vcat[part, :] = vtab[index]
            ktcat[:, part] = kttab[index]
        for g in range(groups):
            cols = slice(g * 2 * block, (g + 1) * 2 * block)
            feats = slice(g * 2 * width, (g + 1) * 2 * width)
            s = dot(kcat[...], qxt[:, cols])
            p = jnp.exp2(s * scale2 - lse_s[:, cols])
            p = jnp.concatenate(
                [
                    p[t * block : (t + 1) * block]
                    if t < LEAST
                    else jnp.where(t < count, p[t * block : (t + 1) * block], 0.0)
                    for t in range(slots)
                ],
                axis=0,
            )
            dp = dot(vcat[...], gxt[:, cols])
            ds = (p * (dp - delta_s[:, cols])).astype(BF16)
            pbuf[:, cols] = p.astype(BF16)
            dsbuf[:, cols] = ds
            o = dot(ktcat[feats, :], ds)
            acc[feats, :] = jnp.concatenate([o[:width, :block], o[width:, block:]], axis=0)
        dv = dot(pbuf[...], gx[...])
        dk = dot(dsbuf[...], qx[...])
        for t in range(slots):
            index = tb_ref[b, t]
            part = slice(t * block, (t + 1) * block)
            dvt[index] += dv[part]
            dkt[index] += dk[part]
        dq_ref[rows, :] = (acc[...] * scale + eq_ref[:, rows]).T
        return carry

    lax.fori_loop(0, blocks, do_block, 0)

    def drain_own(b, carry):
        rows = pl.ds(pl.multiple_of(b * block, block), block)
        dk_ref[rows, :] = dkt[b] * scale
        dv_ref[rows, :] = dvt[b]
        return carry

    def drain_halo(s, carry):
        ret_ref[s, pl.ds(0, block), :] = (dkt[blocks + s] * scale).astype(BF16)
        ret_ref[s, pl.ds(block, block), :] = dvt[blocks + s].astype(BF16)
        return carry

    lax.fori_loop(0, blocks, drain_own, 0)
    lax.fori_loop(0, halo, drain_halo, 0)


def pass_kernel(back_ref, *refs):
    pass


def final_kernel(send_ref, dk_ref, dv_ref, home_ref, *refs, block):
    terms, (ok_ref, ov_ref) = refs[:3], refs[3:]
    nodes = dk_ref.shape[0]
    ok_ref[...] = dk_ref[...] + sum(term[:nodes, :].astype(F32) for term in terms)
    ov_ref[...] = dv_ref[...] + sum(term[nodes:, :].astype(F32) for term in terms)

    def body(s, carry):
        rows = pl.ds(pl.multiple_of(send_ref[s] * block, block), block)
        ok_ref[rows, :] += home_ref[s, pl.ds(0, block), :].astype(F32)
        ov_ref[rows, :] += home_ref[s, pl.ds(block, block), :].astype(F32)
        return carry

    lax.fori_loop(0, home_ref.shape[0], body, 0)


def call(kernel, name, ins, outs, args, scratch=(), estimate=None, mib=16, **static):
    return pl.pallas_call(
        functools.partial(kernel, **static),
        name=name,
        in_specs=ins,
        out_specs=[VMEM] * len(outs),
        out_shape=[jax.ShapeDtypeStruct(shape, dtype) for shape, dtype in outs],
        scratch_shapes=list(scratch),
        compiler_params=params(mib),
        cost_estimate=estimate,
    )(*args)


def from_partner(array, axis, apart):
    return lax.ppermute(array, axis, [(i, i ^ 1 << apart) for i in range(lax.axis_size(axis))])


def reduce_everywhere(term, axes):
    devices = lax.axis_size(axes)
    rows, columns = term.shape
    parts = term.reshape(devices, rows // devices, columns)
    mine = lax.all_to_all(parts, axes, split_axis=0, concat_axis=0, tiled=True).sum(axis=0)
    copies = jnp.broadcast_to(mine[None], parts.shape)
    return lax.all_to_all(copies, axes, split_axis=0, concat_axis=0, tiled=True).reshape(rows, columns)


def shards(
    query_rows, key_rows, value_rows, out_weight, grad_update, expander_bias,
    tile_block, tile_count, send_block, matching,
):
    nodes, feat = query_rows.shape
    heads = expander_bias.shape[0]
    tile_block = tile_block[0]
    tile_count = tile_count[0]
    send_block = send_block[0]
    matching = matching[0]
    blocks, slots = tile_block.shape
    block = nodes // blocks
    halo = send_block.shape[0]
    entries = blocks + halo
    axes = ("group", "dom")
    devices = lax.axis_size(axes)
    top_bit = devices.bit_length() - 1
    wide = heads * block
    tile_flops = 2 * wide * feat * block * blocks * slots

    both = jnp.concatenate([key_rows, value_rows], axis=0)
    moved = [from_partner(both, axes, top_bit - 1 - turn) for turn in range(3)]
    (sent,) = call(
        pick_kernel, "pick", [SMEM, VMEM], [((halo, 2 * block, feat), BF16)],
        (send_block, both), block=block,
        estimate=cost(0, 4 * halo * block * feat * 2),
    )
    got = lax.all_to_all(sent, "dom", split_axis=0, concat_axis=0, tiled=True)
    qt, gat, ga = call(
        prep_kernel, "prep", [VMEM] * 3,
        [((feat, nodes), BF16), ((feat, nodes), BF16), ((nodes, feat), BF16)],
        (query_rows, grad_update, out_weight),
        estimate=cost(2 * nodes * feat * feat, 10 * nodes * feat),
    )
    ot, top, total = call(
        fwd_kernel, "fwd_tiles", [SMEM, SMEM] + [VMEM] * 4,
        [((feat, nodes), F32), ((heads, nodes), F32), ((heads, nodes), F32)],
        (tile_block, tile_count, query_rows, key_rows, value_rows, got),
        scratch=[
            pltpu.VMEM((entries, block, feat), BF16),
            pltpu.VMEM((entries, feat, block), BF16),
            pltpu.VMEM((slots * block, feat), BF16),
            pltpu.VMEM((feat, slots * block), BF16),
            pltpu.VMEM((feat, wide), BF16),
            pltpu.VMEM((1, wide), F32),
            pltpu.VMEM((1, wide), F32),
        ],
        estimate=cost(tile_flops / 2, nodes * feat),
        mib=16 + entries // 4,
        heads=heads, block=block,
    )
    rows = [matching[turn : turn + 1] for turn in range(3)]
    far = [None] * 3
    for turn in range(3):
        far[turn] = call(
            gather_kernel, f"gather{turn}", [VMEM] * 4 + [ANY],
            [((feat, nodes), BF16), ((feat, nodes), BF16), ((heads, nodes), F32), ((heads, nodes), F32)],
            (rows[turn], moved[turn], qt, gat, top),
            estimate=cost(4 * nodes * nodes * feat, 12 * nodes * feat),
            heads=heads,
        )
    merged = call(
        merge_kernel, "merge", [VMEM] * 18,
        [
            ((nodes, feat), BF16), ((feat, nodes), BF16), ((heads, nodes), F32),
            ((heads, nodes), F32), ((feat, nodes), F32),
        ] + [((heads, nodes), F32)] * 6,
        (expander_bias.reshape(heads, 1), ot, top, total, gat, out_weight,
         *far[0], *far[1], *far[2]),
        estimate=cost(4 * nodes * feat * feat, 24 * nodes * feat),
        heads=heads,
    )
    update, attended, lse, delta, edge_query = merged[:5]
    owned, ready = [], []
    for turn in range(3):
        (placed,) = call(
            scatter_kernel, f"scatter{turn}", [VMEM] * 5 + [ANY],
            [((2 * nodes, feat), BF16)],
            (rows[turn], qt, gat, merged[5 + 2 * turn], merged[6 + 2 * turn],
             ready[-1] if ready else lse),
            estimate=cost(4 * nodes * nodes * feat, 10 * nodes * feat),
            heads=heads,
        )
        ready.append(placed)
        owned.append(from_partner(placed, axes, top_bit - 1 - turn))
    (weight_term,) = call(
        weight_kernel, "weight_term", [VMEM, VMEM, ANY], [((feat, feat), F32)],
        (attended, grad_update, ready[-1]),
        estimate=cost(2 * nodes * feat * feat, 4 * nodes * feat), mib=8,
    )
    weight_grad = reduce_everywhere(weight_term, axes) * (nodes * devices) ** (-0.5)
    query_grad, own_k, own_v, back = call(
        bwd_kernel, "bwd_tiles", [SMEM, SMEM] + [VMEM] * 10 + [ANY] * 3,
        [((nodes, feat), F32), ((nodes, feat), F32), ((nodes, feat), F32), ((halo, 2 * block, feat), BF16)],
        (tile_block, tile_count, query_rows, key_rows, value_rows, got, qt, gat, ga,
         lse, delta, edge_query, *ready),
        scratch=[
            pltpu.VMEM((entries, block, feat), BF16),
            pltpu.VMEM((entries, block, feat), BF16),
            pltpu.VMEM((entries, feat, block), BF16),
            pltpu.VMEM((slots * block, feat), BF16),
            pltpu.VMEM((slots * block, feat), BF16),
            pltpu.VMEM((feat, slots * block), BF16),
            pltpu.VMEM((slots * block, wide), BF16),
            pltpu.VMEM((slots * block, wide), BF16),
            pltpu.VMEM((feat, wide), BF16),
            pltpu.VMEM((feat, wide), BF16),
            pltpu.VMEM((wide, feat), BF16),
            pltpu.VMEM((wide, feat), BF16),
            pltpu.VMEM((entries, block, feat), F32),
            pltpu.VMEM((entries, block, feat), F32),
            pltpu.VMEM((feat, block), F32),
            pltpu.VMEM((1, wide), F32),
            pltpu.VMEM((1, wide), F32),
        ],
        estimate=cost(tile_flops / 2, nodes * feat),
        mib=22 + 3 * entries // 5,
        heads=heads, block=block,
    )
    back = pl.pallas_call(
        pass_kernel,
        name="after_terms",
        in_specs=[ANY] * 4,
        out_specs=ANY,
        out_shape=jax.ShapeDtypeStruct(back.shape, back.dtype),
        input_output_aliases={0: 0},
        cost_estimate=cost(0, 0),
    )(back, *owned)
    home = lax.all_to_all(back, "dom", split_axis=0, concat_axis=0, tiled=True)
    key_grad, value_grad = call(
        final_kernel, "final", [SMEM] + [VMEM] * 6,
        [((nodes, feat), F32), ((nodes, feat), F32)],
        (send_block, own_k, own_v, home, *owned),
        estimate=cost(0, 40 * nodes * feat),
        block=block,
    )
    return update, query_grad, key_grad, value_grad, weight_grad


def solution(mesh):
    split = P(("group", "dom"), None)
    split3 = P(("group", "dom"), None, None)
    in_specs = (split, split, split, P(), split, P(), split3, split, split, split3)
    out_specs = (split, split, split, split, P())
    return jax.shard_map(shards, mesh=mesh, in_specs=in_specs, out_specs=out_specs, check_vma=False)
```

```python
import functools
import math

import jax
import jax.numpy as jnp
from jax import lax
from jax.experimental import pallas as pl
from jax.experimental.pallas import tpu as pltpu
from jax.sharding import PartitionSpec as P

LOG2E = math.log2(math.e)
LEAST = 5
VMEM = pl.BlockSpec(memory_space=pltpu.VMEM)
ANY = pl.BlockSpec(memory_space=pl.ANY)
SMEM = pl.BlockSpec(memory_space=pltpu.SMEM)
F32 = jnp.float32
BF16 = jnp.bfloat16


def params(mib):
    return pltpu.CompilerParams(vmem_limit_bytes=mib * 1024 * 1024)


def cost(flops, moved):
    return pl.CostEstimate(flops=int(flops), bytes_accessed=int(moved), transcendentals=0)


def dot(left, right, left_dim=1, right_dim=0):
    return lax.dot_general(
        left, right, (((left_dim,), (right_dim,)), ((), ())), preferred_element_type=F32
    )


def spread(rows, width):
    heads, lanes = rows.shape
    return jnp.concatenate(
        [jnp.broadcast_to(rows[h : h + 1], (width, lanes)) for h in range(heads)], axis=0
    )


def head_sums(product, heads):
    features, lanes = product.shape
    return product.reshape(heads, features // heads, lanes).sum(axis=1)


def pick_kernel(send_ref, both_ref, out_ref, *, block):
    nodes = both_ref.shape[0] // 2

    def body(s, carry):
        start = pl.multiple_of(send_ref[s] * block, block)
        out_ref[s, pl.ds(0, block), :] = both_ref[pl.ds(start, block), :]
        out_ref[s, pl.ds(block, block), :] = both_ref[pl.ds(nodes + start, block), :]
        return carry

    lax.fori_loop(0, out_ref.shape[0], body, 0)


def fwd_kernel(
    tb_ref, tc_ref, q_ref, k_ref, v_ref, got_ref,
    ot_ref, m_ref, l_ref,
    ktab, vttab, kcat, vtcat, qx, m_s, l_s,
    *, heads, block,
):
    nodes, feat = q_ref.shape
    blocks = nodes // block
    halo = got_ref.shape[0]
    width = feat // heads
    scale2 = width**-0.5 * LOG2E
    groups = heads // 2
    slots = tb_ref.shape[1]

    def fill_own(b, carry):
        rows = pl.ds(pl.multiple_of(b * block, block), block)
        ktab[b] = k_ref[rows, :]
        vttab[b] = v_ref[rows, :].T
        return carry

    def fill_halo(s, carry):
        ktab[blocks + s] = got_ref[s, pl.ds(0, block), :]
        vttab[blocks + s] = got_ref[s, pl.ds(block, block), :].T
        return carry

    lax.fori_loop(0, blocks, fill_own, 0)
    lax.fori_loop(0, halo, fill_halo, 0)
    qx[...] = jnp.zeros(qx.shape, qx.dtype)

    def do_block(b, carry):
        rows = pl.ds(pl.multiple_of(b * block, block), block)
        qt = q_ref[rows, :].T
        for h in range(heads):
            qx[h * width : (h + 1) * width, h * block : (h + 1) * block] = qt[
                h * width : (h + 1) * width
            ]
        count = tc_ref[b]
        for t in range(slots):
            index = tb_ref[b, t]
            kcat[t * block : (t + 1) * block, :] = ktab[index]
            vtcat[:, t * block : (t + 1) * block] = vttab[index]
        for g in range(groups):
            cols = slice(g * 2 * block, (g + 1) * 2 * block)
            feats = slice(g * 2 * width, (g + 1) * 2 * width)
            s = dot(kcat[...], qx[:, cols])
            live = [
                s[t * block : (t + 1) * block]
                if t < LEAST
                else jnp.where(t < count, s[t * block : (t + 1) * block], -1e30)
                for t in range(slots)
            ]
            s = jnp.concatenate(live, axis=0)
            top = s.max(axis=0, keepdims=True)
            p = jnp.exp2((s - top) * scale2)
            m_s[:, cols] = top
            l_s[:, cols] = p.sum(axis=0, keepdims=True)
            o = dot(vtcat[feats, :], p.astype(BF16))
            ot_ref[feats, rows] = jnp.concatenate([o[:width, :block], o[width:, block:]], axis=0)
        for h in range(heads):
            m_ref[h : h + 1, rows] = m_s[:, h * block : (h + 1) * block] * (width**-0.5)
            l_ref[h : h + 1, rows] = l_s[:, h * block : (h + 1) * block]
        return carry

    lax.fori_loop(0, blocks, do_block, 0)


def prep_kernel(q_ref, gu_ref, w_ref, qt_ref, gat_ref, ga_ref):
    qt_ref[...] = q_ref[...].T
    ga = dot(gu_ref[...], w_ref[...], 1, 1).astype(BF16)
    ga_ref[...] = ga
    gat_ref[...] = ga.T


def hot(match_row, nodes):
    return (lax.broadcasted_iota(jnp.int32, (nodes, nodes), 0) == match_row).astype(BF16)


def gather_kernel(match_ref, moved_ref, qt_ref, gat_ref, after_ref, fk_ref, fv_ref, s_ref, dp_ref, *, heads):
    nodes = qt_ref.shape[1]
    onehot = hot(match_ref[...], nodes)
    fk = dot(moved_ref[:nodes, :].T, onehot)
    fk_ref[...] = fk.astype(BF16)
    s_ref[...] = head_sums(fk * qt_ref[...].astype(F32), heads)
    fv = dot(moved_ref[nodes:, :].T, onehot)
    fv_ref[...] = fv.astype(BF16)
    dp_ref[...] = head_sums(fv * gat_ref[...].astype(F32), heads)


def merge_kernel(*refs, heads):
    (bias_ref, ot_ref, m_ref, l_ref, gat_ref, gu_ref, w_ref) = refs[:7]
    far = refs[7:19]
    update_ref, term_ref, lse_ref, delta_ref, eq_ref = refs[19:24]
    out = refs[24:]
    feat = ot_ref.shape[0]
    width = feat // heads
    scale = width**-0.5
    scores = [far[4 * e + 2][...] * scale + bias_ref[...] for e in range(3)]
    old = m_ref[...]
    top = functools.reduce(jnp.maximum, scores, old)
    tile_factor = jnp.exp(old - top)
    edge = [jnp.exp(s - top) for s in scores]
    total = l_ref[...] * tile_factor + edge[0] + edge[1] + edge[2]
    probs = [e / total for e in edge]
    weights = [p.astype(BF16).astype(F32) for p in probs]
    mixed = ot_ref[...] * spread(tile_factor / total, width)
    for e in range(3):
        mixed = mixed + spread(weights[e], width) * far[4 * e + 1][...].astype(F32)
    att = mixed.astype(BF16)
    update_ref[...] = dot(att, w_ref[...], 0, 0).astype(BF16)
    term_ref[...] = dot(att, gu_ref[...])
    delta = head_sums(att.astype(F32) * gat_ref[...].astype(F32), heads)
    delta_ref[...] = delta
    lse_ref[...] = top * LOG2E + jnp.log2(total)
    query = None
    for e in range(3):
        ds = (probs[e] * (far[4 * e + 3][...] - delta) * scale).astype(BF16).astype(F32)
        out[2 * e][...] = ds
        out[2 * e + 1][...] = weights[e]
        part = spread(ds, width) * far[4 * e][...].astype(F32)
        query = part if query is None else query + part
    eq_ref[...] = query


def scatter_kernel(match_ref, qt_ref, gat_ref, ds_ref, wt_ref, after_ref, placed_ref, *, heads):
    feat, nodes = qt_ref.shape
    width = feat // heads
    onehot = hot(match_ref[...], nodes)
    kt = (spread(ds_ref[...], width) * qt_ref[...].astype(F32)).astype(BF16)
    placed_ref[:nodes, :] = dot(onehot, kt, 1, 1).astype(BF16)
    vt = (spread(wt_ref[...], width) * gat_ref[...].astype(F32)).astype(BF16)
    placed_ref[nodes:, :] = dot(onehot, vt, 1, 1).astype(BF16)


def bwd_kernel(
    tb_ref, tc_ref, q_ref, k_ref, v_ref, got_ref, qt_ref, gat_ref, ga_ref,
    lse_ref, delta_ref, eq_ref, after0_ref, after1_ref, after2_ref,
    dq_ref, dk_ref, dv_ref, ret_ref,
    ktab, vtab, kttab, kcat, vcat, ktcat, pbuf, dsbuf, qxt, gxt, qx, gx, dkt, dvt, acc, lse_s, delta_s,
    *, heads, block,
):
    nodes, feat = q_ref.shape
    blocks = nodes // block
    halo = got_ref.shape[0]
    width = feat // heads
    scale = width**-0.5
    scale2 = scale * LOG2E
    groups = heads // 2
    slots = tb_ref.shape[1]

    def fill_own(b, carry):
        rows = pl.ds(pl.multiple_of(b * block, block), block)
        k = k_ref[rows, :]
        ktab[b] = k
        kttab[b] = k.T
        vtab[b] = v_ref[rows, :]
        return carry

    def fill_halo(s, carry):
        k = got_ref[s, pl.ds(0, block), :]
        ktab[blocks + s] = k
        kttab[blocks + s] = k.T
        vtab[blocks + s] = got_ref[s, pl.ds(block, block), :]
        return carry

    def clear(e, carry):
        dkt[e] = jnp.zeros((block, feat), F32)
        dvt[e] = jnp.zeros((block, feat), F32)
        return carry

    lax.fori_loop(0, blocks, fill_own, 0)
    lax.fori_loop(0, halo, fill_halo, 0)
    lax.fori_loop(0, blocks + halo, clear, 0)
    qxt[...] = jnp.zeros(qxt.shape, qxt.dtype)
    gxt[...] = jnp.zeros(gxt.shape, gxt.dtype)

    def do_block(b, carry):
        rows = pl.ds(pl.multiple_of(b * block, block), block)
        lanes = lax.broadcasted_iota(jnp.int32, (block, feat), 1) // width
        qf = q_ref[rows, :].astype(F32)
        gf = ga_ref[rows, :].astype(F32)
        qt = qt_ref[:, rows]
        gt = gat_ref[:, rows]
        for h in range(heads):
            hs, bs = slice(h * width, (h + 1) * width), slice(h * block, (h + 1) * block)
            qxt[hs, bs] = qt[hs]
            gxt[hs, bs] = gt[hs]
            qx[bs, :] = jnp.where(lanes == h, qf, 0.0).astype(BF16)
            gx[bs, :] = jnp.where(lanes == h, gf, 0.0).astype(BF16)
            lse_s[:, bs] = lse_ref[h : h + 1, rows]
            delta_s[:, bs] = delta_ref[h : h + 1, rows]

        count = tc_ref[b]

        for t in range(slots):
            index = tb_ref[b, t]
            part = slice(t * block, (t + 1) * block)
            kcat[part, :] = ktab[index]
            vcat[part, :] = vtab[index]
            ktcat[:, part] = kttab[index]
        for g in range(groups):
            cols = slice(g * 2 * block, (g + 1) * 2 * block)
            feats = slice(g * 2 * width, (g + 1) * 2 * width)
            s = dot(kcat[...], qxt[:, cols])
            p = jnp.exp2(s * scale2 - lse_s[:, cols])
            p = jnp.concatenate(
                [
                    p[t * block : (t + 1) * block]
                    if t < LEAST
                    else jnp.where(t < count, p[t * block : (t + 1) * block], 0.0)
                    for t in range(slots)
                ],
                axis=0,
            )
            dp = dot(vcat[...], gxt[:, cols])
            ds = (p * (dp - delta_s[:, cols])).astype(BF16)
            pbuf[:, cols] = p.astype(BF16)
            dsbuf[:, cols] = ds
            o = dot(ktcat[feats, :], ds)
            acc[feats, :] = jnp.concatenate([o[:width, :block], o[width:, block:]], axis=0)
        dv = dot(pbuf[...], gx[...])
        dk = dot(dsbuf[...], qx[...])
        for t in range(slots):
            index = tb_ref[b, t]
            part = slice(t * block, (t + 1) * block)
            dvt[index] += dv[part]
            dkt[index] += dk[part]
        dq_ref[rows, :] = (acc[...] * scale + eq_ref[:, rows]).T
        return carry

    lax.fori_loop(0, blocks, do_block, 0)

    def drain_own(b, carry):
        rows = pl.ds(pl.multiple_of(b * block, block), block)
        dk_ref[rows, :] = dkt[b] * scale
        dv_ref[rows, :] = dvt[b]
        return carry

    def drain_halo(s, carry):
        ret_ref[s, pl.ds(0, block), :] = (dkt[blocks + s] * scale).astype(BF16)
        ret_ref[s, pl.ds(block, block), :] = dvt[blocks + s].astype(BF16)
        return carry

    lax.fori_loop(0, blocks, drain_own, 0)
    lax.fori_loop(0, halo, drain_halo, 0)


def pass_kernel(back_ref, *refs):
    pass


def final_kernel(send_ref, dk_ref, dv_ref, home_ref, *refs, block):
    terms, (ok_ref, ov_ref) = refs[:3], refs[3:]
    nodes = dk_ref.shape[0]
    ok_ref[...] = dk_ref[...] + sum(term[:nodes, :].astype(F32) for term in terms)
    ov_ref[...] = dv_ref[...] + sum(term[nodes:, :].astype(F32) for term in terms)

    def body(s, carry):
        rows = pl.ds(pl.multiple_of(send_ref[s] * block, block), block)
        ok_ref[rows, :] += home_ref[s, pl.ds(0, block), :].astype(F32)
        ov_ref[rows, :] += home_ref[s, pl.ds(block, block), :].astype(F32)
        return carry

    lax.fori_loop(0, home_ref.shape[0], body, 0)


def origin(dims, step):
    return (0,) * dims


def call(kernel, name, ins, outs, args, scratch=(), estimate=None, mib=16, whole=False, **static):
    if whole:
        ins = [
            pl.BlockSpec(
                arg.shape, functools.partial(origin, arg.ndim), pipeline_mode=pl.Buffered(1)
            )
            if spec is VMEM
            else spec
            for spec, arg in zip(ins, args)
        ]
        out_specs = [
            pl.BlockSpec(shape, functools.partial(origin, len(shape))) for shape, _ in outs
        ]
    else:
        out_specs = [VMEM] * len(outs)
    return pl.pallas_call(
        functools.partial(kernel, **static),
        name=name,
        grid=(1,) if whole else (),
        in_specs=ins,
        out_specs=out_specs,
        out_shape=[jax.ShapeDtypeStruct(shape, dtype) for shape, dtype in outs],
        scratch_shapes=list(scratch),
        compiler_params=params(mib),
        cost_estimate=estimate,
    )(*args)


def from_partner(array, axis, apart):
    return lax.ppermute(array, axis, [(i, i ^ 1 << apart) for i in range(lax.axis_size(axis))])


def reduce_everywhere(term, axes):
    devices = lax.axis_size(axes)
    rows, columns = term.shape
    parts = term.reshape(devices, rows // devices, columns)
    mine = lax.all_to_all(parts, axes, split_axis=0, concat_axis=0, tiled=True).sum(axis=0)
    copies = jnp.broadcast_to(mine[None], parts.shape)
    return lax.all_to_all(copies, axes, split_axis=0, concat_axis=0, tiled=True).reshape(rows, columns)


def shards(
    query_rows, key_rows, value_rows, out_weight, grad_update, expander_bias,
    tile_block, tile_count, send_block, matching,
):
    nodes, feat = query_rows.shape
    heads = expander_bias.shape[0]
    tile_block = tile_block[0]
    tile_count = tile_count[0]
    send_block = send_block[0]
    matching = matching[0]
    blocks, slots = tile_block.shape
    block = nodes // blocks
    halo = send_block.shape[0]
    entries = blocks + halo
    axes = ("group", "dom")
    devices = lax.axis_size(axes)
    top_bit = devices.bit_length() - 1
    wide = heads * block
    tile_flops = 2 * wide * feat * block * blocks * slots

    both = jnp.concatenate([key_rows, value_rows], axis=0)
    moved = [from_partner(both, axes, top_bit - 1 - turn) for turn in range(3)]
    (sent,) = call(
        pick_kernel, "pick", [SMEM, VMEM], [((halo, 2 * block, feat), BF16)],
        (send_block, both), block=block,
        estimate=cost(0, 4 * halo * block * feat * 2),
    )
    got = lax.all_to_all(sent, "dom", split_axis=0, concat_axis=0, tiled=True)
    qt, gat, ga = call(
        prep_kernel, "prep", [VMEM] * 3,
        [((feat, nodes), BF16), ((feat, nodes), BF16), ((nodes, feat), BF16)],
        (query_rows, grad_update, out_weight),
        estimate=cost(2 * nodes * feat * feat, 10 * nodes * feat),
    )
    ot, top, total = call(
        fwd_kernel, "fwd_tiles", [SMEM, SMEM] + [VMEM] * 4,
        [((feat, nodes), F32), ((heads, nodes), F32), ((heads, nodes), F32)],
        (tile_block, tile_count, query_rows, key_rows, value_rows, got),
        scratch=[
            pltpu.VMEM((entries, block, feat), BF16),
            pltpu.VMEM((entries, feat, block), BF16),
            pltpu.VMEM((slots * block, feat), BF16),
            pltpu.VMEM((feat, slots * block), BF16),
            pltpu.VMEM((feat, wide), BF16),
            pltpu.VMEM((1, wide), F32),
            pltpu.VMEM((1, wide), F32),
        ],
        estimate=cost(tile_flops / 2, nodes * feat),
        mib=20 + entries // 2, whole=True,
        heads=heads, block=block,
    )
    rows = [matching[turn : turn + 1] for turn in range(3)]
    far = [None] * 3
    for turn in range(3):
        far[turn] = call(
            gather_kernel, f"gather{turn}", [VMEM] * 4 + [ANY],
            [((feat, nodes), BF16), ((feat, nodes), BF16), ((heads, nodes), F32), ((heads, nodes), F32)],
            (rows[turn], moved[turn], qt, gat, top),
            estimate=cost(4 * nodes * nodes * feat, 12 * nodes * feat),
            heads=heads,
        )
    merged = call(
        merge_kernel, "merge", [VMEM] * 19,
        [
            ((nodes, feat), BF16), ((feat, feat), F32), ((heads, nodes), F32),
            ((heads, nodes), F32), ((feat, nodes), F32),
        ] + [((heads, nodes), F32)] * 6,
        (expander_bias.reshape(heads, 1), ot, top, total, gat, grad_update, out_weight,
         *far[0], *far[1], *far[2]),
        estimate=cost(4 * nodes * feat * feat, 24 * nodes * feat),
        heads=heads,
    )
    update, weight_term, lse, delta, edge_query = merged[:5]
    owned, ready = [], []
    for turn in range(3):
        (placed,) = call(
            scatter_kernel, f"scatter{turn}", [VMEM] * 5 + [ANY],
            [((2 * nodes, feat), BF16)],
            (rows[turn], qt, gat, merged[5 + 2 * turn], merged[6 + 2 * turn],
             ready[-1] if ready else lse),
            estimate=cost(4 * nodes * nodes * feat, 10 * nodes * feat),
            heads=heads,
        )
        ready.append(placed)
        owned.append(from_partner(placed, axes, top_bit - 1 - turn))
    weight_grad = reduce_everywhere(weight_term, axes) * (nodes * devices) ** (-0.5)
    query_grad, own_k, own_v, back = call(
        bwd_kernel, "bwd_tiles", [SMEM, SMEM] + [VMEM] * 10 + [ANY] * 3,
        [((nodes, feat), F32), ((nodes, feat), F32), ((nodes, feat), F32), ((halo, 2 * block, feat), BF16)],
        (tile_block, tile_count, query_rows, key_rows, value_rows, got, qt, gat, ga,
         lse, delta, edge_query, *ready),
        scratch=[
            pltpu.VMEM((entries, block, feat), BF16),
            pltpu.VMEM((entries, block, feat), BF16),
            pltpu.VMEM((entries, feat, block), BF16),
            pltpu.VMEM((slots * block, feat), BF16),
            pltpu.VMEM((slots * block, feat), BF16),
            pltpu.VMEM((feat, slots * block), BF16),
            pltpu.VMEM((slots * block, wide), BF16),
            pltpu.VMEM((slots * block, wide), BF16),
            pltpu.VMEM((feat, wide), BF16),
            pltpu.VMEM((feat, wide), BF16),
            pltpu.VMEM((wide, feat), BF16),
            pltpu.VMEM((wide, feat), BF16),
            pltpu.VMEM((entries, block, feat), F32),
            pltpu.VMEM((entries, block, feat), F32),
            pltpu.VMEM((feat, block), F32),
            pltpu.VMEM((1, wide), F32),
            pltpu.VMEM((1, wide), F32),
        ],
        estimate=cost(tile_flops / 2, nodes * feat),
        mib=30 + 2 * entries // 3, whole=True,
        heads=heads, block=block,
    )
    back = pl.pallas_call(
        pass_kernel,
        name="after_terms",
        in_specs=[ANY] * 4,
        out_specs=ANY,
        out_shape=jax.ShapeDtypeStruct(back.shape, back.dtype),
        input_output_aliases={0: 0},
        cost_estimate=cost(0, 0),
    )(back, *owned)
    home = lax.all_to_all(back, "dom", split_axis=0, concat_axis=0, tiled=True)
    key_grad, value_grad = call(
        final_kernel, "final", [SMEM] + [VMEM] * 6,
        [((nodes, feat), F32), ((nodes, feat), F32)],
        (send_block, own_k, own_v, home, *owned),
        estimate=cost(0, 40 * nodes * feat),
        mib=24 + entries // 2, whole=True, block=block,
    )
    return update, query_grad, key_grad, value_grad, weight_grad


def solution(mesh):
    split = P(("group", "dom"), None)
    split3 = P(("group", "dom"), None, None)
    in_specs = (split, split, split, P(), split, P(), split3, split, split, split3)
    out_specs = (split, split, split, split, P())
    return jax.shard_map(shards, mesh=mesh, in_specs=in_specs, out_specs=out_specs, check_vma=False)
```

```python
import functools
import math

import jax
import jax.numpy as jnp
from jax import lax
from jax.experimental import pallas as pl
from jax.experimental.pallas import tpu as pltpu
from jax.sharding import PartitionSpec as P

LOG2E = math.log2(math.e)
LEAST = 5
VMEM = pl.BlockSpec(memory_space=pltpu.VMEM)
ANY = pl.BlockSpec(memory_space=pl.ANY)
SMEM = pl.BlockSpec(memory_space=pltpu.SMEM)
F32 = jnp.float32
BF16 = jnp.bfloat16


def params(mib):
    return pltpu.CompilerParams(vmem_limit_bytes=mib * 1024 * 1024)


def cost(flops, moved):
    return pl.CostEstimate(flops=int(flops), bytes_accessed=int(moved), transcendentals=0)


def dot(left, right, left_dim=1, right_dim=0):
    return lax.dot_general(
        left, right, (((left_dim,), (right_dim,)), ((), ())), preferred_element_type=F32
    )


def spread(rows, width):
    heads, lanes = rows.shape
    return jnp.concatenate(
        [jnp.broadcast_to(rows[h : h + 1], (width, lanes)) for h in range(heads)], axis=0
    )


def head_sums(product, heads):
    features, lanes = product.shape
    return product.reshape(heads, features // heads, lanes).sum(axis=1)


def pick_kernel(send_ref, both_ref, out_ref, *, block):
    nodes = both_ref.shape[0] // 2

    def body(s, carry):
        start = pl.multiple_of(send_ref[s] * block, block)
        out_ref[s, pl.ds(0, block), :] = both_ref[pl.ds(start, block), :]
        out_ref[s, pl.ds(block, block), :] = both_ref[pl.ds(nodes + start, block), :]
        return carry

    lax.fori_loop(0, out_ref.shape[0], body, 0)


def fwd_kernel(
    tb_ref, tc_ref, q_ref, k_ref, v_ref, got_ref,
    ot_ref, m_ref, l_ref,
    ktab, vttab, kcat, vtcat, qx, m_s, l_s,
    *, heads, block,
):
    nodes, feat = q_ref.shape
    blocks = nodes // block
    halo = got_ref.shape[0]
    width = feat // heads
    scale2 = width**-0.5 * LOG2E
    groups = heads // 2
    slots = tb_ref.shape[1]

    def fill_own(b, carry):
        rows = pl.ds(pl.multiple_of(b * block, block), block)
        ktab[b] = k_ref[rows, :]
        vttab[b] = v_ref[rows, :].T
        return carry

    def fill_halo(s, carry):
        ktab[blocks + s] = got_ref[s, pl.ds(0, block), :]
        vttab[blocks + s] = got_ref[s, pl.ds(block, block), :].T
        return carry

    lax.fori_loop(0, blocks, fill_own, 0)
    lax.fori_loop(0, halo, fill_halo, 0)
    qx[...] = jnp.zeros(qx.shape, qx.dtype)

    def do_block(b, carry):
        rows = pl.ds(pl.multiple_of(b * block, block), block)
        qt = q_ref[rows, :].T
        for h in range(heads):
            qx[h * width : (h + 1) * width, h * block : (h + 1) * block] = qt[
                h * width : (h + 1) * width
            ]
        count = tc_ref[b]
        for t in range(slots):
            index = tb_ref[b, t]
            kcat[t * block : (t + 1) * block, :] = ktab[index]
            vtcat[:, t * block : (t + 1) * block] = vttab[index]
        for g in range(groups):
            cols = slice(g * 2 * block, (g + 1) * 2 * block)
            feats = slice(g * 2 * width, (g + 1) * 2 * width)
            s = dot(kcat[...], qx[:, cols])
            live = [
                s[t * block : (t + 1) * block]
                if t < LEAST
                else jnp.where(t < count, s[t * block : (t + 1) * block], -1e30)
                for t in range(slots)
            ]
            s = jnp.concatenate(live, axis=0)
            top = s.max(axis=0, keepdims=True)
            p = jnp.exp2((s - top) * scale2)
            m_s[:, cols] = top
            l_s[:, cols] = p.sum(axis=0, keepdims=True)
            o = dot(vtcat[feats, :], p.astype(BF16))
            ot_ref[feats, rows] = jnp.concatenate([o[:width, :block], o[width:, block:]], axis=0)
        for h in range(heads):
            m_ref[h : h + 1, rows] = m_s[:, h * block : (h + 1) * block] * (width**-0.5)
            l_ref[h : h + 1, rows] = l_s[:, h * block : (h + 1) * block]
        return carry

    lax.fori_loop(0, blocks, do_block, 0)


def prep_kernel(q_ref, gu_ref, w_ref, qt_ref, gat_ref, ga_ref):
    qt_ref[...] = q_ref[...].T
    ga = dot(gu_ref[...], w_ref[...], 1, 1).astype(BF16)
    ga_ref[...] = ga
    gat_ref[...] = ga.T


def hot(match_row, nodes):
    return (lax.broadcasted_iota(jnp.int32, (nodes, nodes), 0) == match_row).astype(BF16)


def gather_kernel(match_ref, moved_ref, qt_ref, gat_ref, after_ref, fk_ref, fv_ref, s_ref, dp_ref, *, heads):
    nodes = qt_ref.shape[1]
    onehot = hot(match_ref[...], nodes)
    fk = dot(moved_ref[:nodes, :].T, onehot)
    fk_ref[...] = fk.astype(BF16)
    s_ref[...] = head_sums(fk * qt_ref[...].astype(F32), heads)
    fv = dot(moved_ref[nodes:, :].T, onehot)
    fv_ref[...] = fv.astype(BF16)
    dp_ref[...] = head_sums(fv * gat_ref[...].astype(F32), heads)


def merge_kernel(*refs, heads):
    (bias_ref, ot_ref, m_ref, l_ref, gat_ref, gu_ref, w_ref) = refs[:7]
    far = refs[7:19]
    update_ref, term_ref, lse_ref, delta_ref, eq_ref = refs[19:24]
    out = refs[24:]
    feat = ot_ref.shape[0]
    width = feat // heads
    scale = width**-0.5
    scores = [far[4 * e + 2][...] * scale + bias_ref[...] for e in range(3)]
    old = m_ref[...]
    top = functools.reduce(jnp.maximum, scores, old)
    tile_factor = jnp.exp(old - top)
    edge = [jnp.exp(s - top) for s in scores]
    total = l_ref[...] * tile_factor + edge[0] + edge[1] + edge[2]
    probs = [e / total for e in edge]
    weights = [p.astype(BF16).astype(F32) for p in probs]
    mixed = ot_ref[...] * spread(tile_factor / total, width)
    for e in range(3):
        mixed = mixed + spread(weights[e], width) * far[4 * e + 1][...].astype(F32)
    att = mixed.astype(BF16)
    update_ref[...] = dot(att, w_ref[...], 0, 0).astype(BF16)
    term_ref[...] = dot(att, gu_ref[...])
    delta = head_sums(att.astype(F32) * gat_ref[...].astype(F32), heads)
    delta_ref[...] = delta
    lse_ref[...] = top * LOG2E + jnp.log2(total)
    query = None
    for e in range(3):
        ds = (probs[e] * (far[4 * e + 3][...] - delta) * scale).astype(BF16).astype(F32)
        out[2 * e][...] = ds
        out[2 * e + 1][...] = weights[e]
        part = spread(ds, width) * far[4 * e][...].astype(F32)
        query = part if query is None else query + part
    eq_ref[...] = query


def scatter_kernel(match_ref, qt_ref, gat_ref, ds_ref, wt_ref, placed_ref, *, heads):
    feat, nodes = qt_ref.shape
    width = feat // heads
    onehot = hot(match_ref[...], nodes)
    kt = (spread(ds_ref[...], width) * qt_ref[...].astype(F32)).astype(BF16)
    placed_ref[:nodes, :] = dot(onehot, kt, 1, 1).astype(BF16)
    vt = (spread(wt_ref[...], width) * gat_ref[...].astype(F32)).astype(BF16)
    placed_ref[nodes:, :] = dot(onehot, vt, 1, 1).astype(BF16)


def bwd_kernel(
    tb_ref, tc_ref, q_ref, k_ref, v_ref, got_ref, qt_ref, gat_ref, ga_ref,
    lse_ref, delta_ref, eq_ref, after0_ref, after1_ref, after2_ref,
    dq_ref, dk_ref, dv_ref, ret_ref,
    ktab, vtab, kttab, kcat, vcat, ktcat, pbuf, dsbuf, qxt, gxt, qx, gx, dkt, dvt, acc, lse_s, delta_s,
    *, heads, block,
):
    nodes, feat = q_ref.shape
    blocks = nodes // block
    halo = got_ref.shape[0]
    width = feat // heads
    scale = width**-0.5
    scale2 = scale * LOG2E
    groups = heads // 2
    slots = tb_ref.shape[1]

    def fill_own(b, carry):
        rows = pl.ds(pl.multiple_of(b * block, block), block)
        k = k_ref[rows, :]
        ktab[b] = k
        kttab[b] = k.T
        vtab[b] = v_ref[rows, :]
        return carry

    def fill_halo(s, carry):
        k = got_ref[s, pl.ds(0, block), :]
        ktab[blocks + s] = k
        kttab[blocks + s] = k.T
        vtab[blocks + s] = got_ref[s, pl.ds(block, block), :]
        return carry

    def clear(e, carry):
        dkt[e] = jnp.zeros((block, feat), F32)
        dvt[e] = jnp.zeros((block, feat), F32)
        return carry

    lax.fori_loop(0, blocks, fill_own, 0)
    lax.fori_loop(0, halo, fill_halo, 0)
    lax.fori_loop(0, blocks + halo, clear, 0)
    qxt[...] = jnp.zeros(qxt.shape, qxt.dtype)
    gxt[...] = jnp.zeros(gxt.shape, gxt.dtype)

    def do_block(b, carry):
        rows = pl.ds(pl.multiple_of(b * block, block), block)
        lanes = lax.broadcasted_iota(jnp.int32, (block, feat), 1) // width
        qf = q_ref[rows, :].astype(F32)
        gf = ga_ref[rows, :].astype(F32)
        qt = qt_ref[:, rows]
        gt = gat_ref[:, rows]
        for h in range(heads):
            hs, bs = slice(h * width, (h + 1) * width), slice(h * block, (h + 1) * block)
            qxt[hs, bs] = qt[hs]
            gxt[hs, bs] = gt[hs]
            qx[bs, :] = jnp.where(lanes == h, qf, 0.0).astype(BF16)
            gx[bs, :] = jnp.where(lanes == h, gf, 0.0).astype(BF16)
            lse_s[:, bs] = lse_ref[h : h + 1, rows]
            delta_s[:, bs] = delta_ref[h : h + 1, rows]

        count = tc_ref[b]

        for t in range(slots):
            index = tb_ref[b, t]
            part = slice(t * block, (t + 1) * block)
            kcat[part, :] = ktab[index]
            vcat[part, :] = vtab[index]
            ktcat[:, part] = kttab[index]
        for g in range(groups):
            cols = slice(g * 2 * block, (g + 1) * 2 * block)
            feats = slice(g * 2 * width, (g + 1) * 2 * width)
            s = dot(kcat[...], qxt[:, cols])
            p = jnp.exp2(s * scale2 - lse_s[:, cols])
            p = jnp.concatenate(
                [
                    p[t * block : (t + 1) * block]
                    if t < LEAST
                    else jnp.where(t < count, p[t * block : (t + 1) * block], 0.0)
                    for t in range(slots)
                ],
                axis=0,
            )
            dp = dot(vcat[...], gxt[:, cols])
            ds = (p * (dp - delta_s[:, cols])).astype(BF16)
            pbuf[:, cols] = p.astype(BF16)
            dsbuf[:, cols] = ds
            o = dot(ktcat[feats, :], ds)
            acc[feats, :] = jnp.concatenate([o[:width, :block], o[width:, block:]], axis=0)
        dv = dot(pbuf[...], gx[...])
        dk = dot(dsbuf[...], qx[...])
        for t in range(slots):
            index = tb_ref[b, t]
            part = slice(t * block, (t + 1) * block)
            dvt[index] += dv[part]
            dkt[index] += dk[part]
        dq_ref[rows, :] = (acc[...] * scale + eq_ref[:, rows]).T
        return carry

    lax.fori_loop(0, blocks, do_block, 0)

    def drain_own(b, carry):
        rows = pl.ds(pl.multiple_of(b * block, block), block)
        dk_ref[rows, :] = dkt[b] * scale
        dv_ref[rows, :] = dvt[b]
        return carry

    def drain_halo(s, carry):
        ret_ref[s, pl.ds(0, block), :] = (dkt[blocks + s] * scale).astype(BF16)
        ret_ref[s, pl.ds(block, block), :] = dvt[blocks + s].astype(BF16)
        return carry

    lax.fori_loop(0, blocks, drain_own, 0)
    lax.fori_loop(0, halo, drain_halo, 0)


def pass_kernel(back_ref, *refs):
    pass


def final_kernel(send_ref, dk_ref, dv_ref, home_ref, *refs, block):
    terms, (ok_ref, ov_ref) = refs[:3], refs[3:]
    nodes = dk_ref.shape[0]
    ok_ref[...] = dk_ref[...] + sum(term[:nodes, :].astype(F32) for term in terms)
    ov_ref[...] = dv_ref[...] + sum(term[nodes:, :].astype(F32) for term in terms)

    def body(s, carry):
        rows = pl.ds(pl.multiple_of(send_ref[s] * block, block), block)
        ok_ref[rows, :] += home_ref[s, pl.ds(0, block), :].astype(F32)
        ov_ref[rows, :] += home_ref[s, pl.ds(block, block), :].astype(F32)
        return carry

    lax.fori_loop(0, home_ref.shape[0], body, 0)


def origin(dims, step):
    return (0,) * dims


def call(kernel, name, ins, outs, args, scratch=(), estimate=None, mib=48, whole=False, **static):
    if whole:
        ins = [
            pl.BlockSpec(
                arg.shape, functools.partial(origin, arg.ndim), pipeline_mode=pl.Buffered(1)
            )
            if spec is VMEM
            else spec
            for spec, arg in zip(ins, args)
        ]
        out_specs = [
            pl.BlockSpec(shape, functools.partial(origin, len(shape))) for shape, _ in outs
        ]
    else:
        out_specs = [VMEM] * len(outs)
    return pl.pallas_call(
        functools.partial(kernel, **static),
        name=name,
        grid=(1,) if whole else (),
        in_specs=ins,
        out_specs=out_specs,
        out_shape=[jax.ShapeDtypeStruct(shape, dtype) for shape, dtype in outs],
        scratch_shapes=list(scratch),
        compiler_params=params(mib),
        cost_estimate=estimate,
    )(*args)


def from_partner(array, axis, apart):
    return lax.ppermute(array, axis, [(i, i ^ 1 << apart) for i in range(lax.axis_size(axis))])


def reduce_everywhere(term, axes):
    devices = lax.axis_size(axes)
    rows, columns = term.shape
    parts = term.reshape(devices, rows // devices, columns)
    mine = lax.all_to_all(parts, axes, split_axis=0, concat_axis=0, tiled=True).sum(axis=0)
    copies = jnp.broadcast_to(mine[None], parts.shape)
    return lax.all_to_all(copies, axes, split_axis=0, concat_axis=0, tiled=True).reshape(rows, columns)


def shards(
    query_rows, key_rows, value_rows, out_weight, grad_update, expander_bias,
    tile_block, tile_count, send_block, matching,
):
    nodes, feat = query_rows.shape
    heads = expander_bias.shape[0]
    tile_block = tile_block[0]
    tile_count = tile_count[0]
    send_block = send_block[0]
    matching = matching[0]
    blocks, slots = tile_block.shape
    block = nodes // blocks
    halo = send_block.shape[0]
    entries = blocks + halo
    axes = ("group", "dom")
    devices = lax.axis_size(axes)
    top_bit = devices.bit_length() - 1
    wide = heads * block
    tile_flops = 2 * wide * feat * block * blocks * slots

    both = jnp.concatenate([key_rows, value_rows], axis=0)
    moved = [from_partner(both, axes, top_bit - 1 - turn) for turn in range(3)]
    (sent,) = call(
        pick_kernel, "pick", [SMEM, VMEM], [((halo, 2 * block, feat), BF16)],
        (send_block, both), block=block,
        estimate=cost(0, 4 * halo * block * feat * 2),
    )
    got = lax.all_to_all(sent, "dom", split_axis=0, concat_axis=0, tiled=True)
    qt, gat, ga = call(
        prep_kernel, "prep", [VMEM] * 3,
        [((feat, nodes), BF16), ((feat, nodes), BF16), ((nodes, feat), BF16)],
        (query_rows, grad_update, out_weight),
        estimate=cost(2 * nodes * feat * feat, 10 * nodes * feat),
    )
    ot, top, total = call(
        fwd_kernel, "fwd_tiles", [SMEM, SMEM] + [VMEM] * 4,
        [((feat, nodes), F32), ((heads, nodes), F32), ((heads, nodes), F32)],
        (tile_block, tile_count, query_rows, key_rows, value_rows, got),
        scratch=[
            pltpu.VMEM((entries, block, feat), BF16),
            pltpu.VMEM((entries, feat, block), BF16),
            pltpu.VMEM((slots * block, feat), BF16),
            pltpu.VMEM((feat, slots * block), BF16),
            pltpu.VMEM((feat, wide), BF16),
            pltpu.VMEM((1, wide), F32),
            pltpu.VMEM((1, wide), F32),
        ],
        estimate=cost(tile_flops / 2, nodes * feat),
        mib=60, whole=True,
        heads=heads, block=block,
    )
    rows = [matching[turn : turn + 1] for turn in range(3)]
    far = [None] * 3
    for turn in range(3):
        far[turn] = call(
            gather_kernel, f"gather{turn}", [VMEM] * 4 + [ANY],
            [((feat, nodes), BF16), ((feat, nodes), BF16), ((heads, nodes), F32), ((heads, nodes), F32)],
            (rows[turn], moved[turn], qt, gat, top),
            estimate=cost(4 * nodes * nodes * feat, 12 * nodes * feat),
            heads=heads,
        )
    merged = call(
        merge_kernel, "merge", [VMEM] * 19,
        [
            ((nodes, feat), BF16), ((feat, feat), F32), ((heads, nodes), F32),
            ((heads, nodes), F32), ((feat, nodes), F32),
        ] + [((heads, nodes), F32)] * 6,
        (expander_bias.reshape(heads, 1), ot, top, total, gat, grad_update, out_weight,
         *far[0], *far[1], *far[2]),
        estimate=cost(4 * nodes * feat * feat, 24 * nodes * feat),
        heads=heads,
    )
    update, weight_term, lse, delta, edge_query = merged[:5]
    owned, ready = [], []
    for turn in range(3):
        (placed,) = call(
            scatter_kernel, f"scatter{turn}", [VMEM] * 5,
            [((2 * nodes, feat), BF16)],
            (rows[turn], qt, gat, merged[5 + 2 * turn], merged[6 + 2 * turn]),
            estimate=cost(4 * nodes * nodes * feat, 10 * nodes * feat),
            heads=heads,
        )
        ready.append(placed)
        owned.append(from_partner(placed, axes, top_bit - 1 - turn))
    weight_grad = reduce_everywhere(weight_term, axes) * (nodes * devices) ** (-0.5)
    query_grad, own_k, own_v, back = call(
        bwd_kernel, "bwd_tiles", [SMEM, SMEM] + [VMEM] * 10 + [ANY] * 3,
        [((nodes, feat), F32), ((nodes, feat), F32), ((nodes, feat), F32), ((halo, 2 * block, feat), BF16)],
        (tile_block, tile_count, query_rows, key_rows, value_rows, got, qt, gat, ga,
         lse, delta, edge_query, *ready),
        scratch=[
            pltpu.VMEM((entries, block, feat), BF16),
            pltpu.VMEM((entries, block, feat), BF16),
            pltpu.VMEM((entries, feat, block), BF16),
            pltpu.VMEM((slots * block, feat), BF16),
            pltpu.VMEM((slots * block, feat), BF16),
            pltpu.VMEM((feat, slots * block), BF16),
            pltpu.VMEM((slots * block, wide), BF16),
            pltpu.VMEM((slots * block, wide), BF16),
            pltpu.VMEM((feat, wide), BF16),
            pltpu.VMEM((feat, wide), BF16),
            pltpu.VMEM((wide, feat), BF16),
            pltpu.VMEM((wide, feat), BF16),
            pltpu.VMEM((entries, block, feat), F32),
            pltpu.VMEM((entries, block, feat), F32),
            pltpu.VMEM((feat, block), F32),
            pltpu.VMEM((1, wide), F32),
            pltpu.VMEM((1, wide), F32),
        ],
        estimate=cost(tile_flops / 2, nodes * feat),
        mib=60, whole=True,
        heads=heads, block=block,
    )
    back = pl.pallas_call(
        pass_kernel,
        name="after_terms",
        in_specs=[ANY] * 4,
        out_specs=ANY,
        out_shape=jax.ShapeDtypeStruct(back.shape, back.dtype),
        input_output_aliases={0: 0},
        cost_estimate=cost(0, 0),
    )(back, *owned)
    home = lax.all_to_all(back, "dom", split_axis=0, concat_axis=0, tiled=True)
    key_grad, value_grad = call(
        final_kernel, "final", [SMEM] + [VMEM] * 6,
        [((nodes, feat), F32), ((nodes, feat), F32)],
        (send_block, own_k, own_v, home, *owned),
        estimate=cost(0, 40 * nodes * feat),
        mib=60, whole=True, block=block,
    )
    return update, query_grad, key_grad, value_grad, weight_grad


def solution(mesh):
    split = P(("group", "dom"), None)
    split3 = P(("group", "dom"), None, None)
    in_specs = (split, split, split, P(), split, P(), split3, split, split, split3)
    out_specs = (split, split, split, split, P())
    return jax.shard_map(shards, mesh=mesh, in_specs=in_specs, out_specs=out_specs, check_vma=False)
```
